512 devices in a mesh: seq: 64 (over y, x, core), grp: 8 (over z).
Axes of the slice: x: 4, y: 8, z: 8, core: 2. Of those that a mesh axis runs over, the one named last changes fastest.
Arguments:
- query: bfloat16 [65536, 4096], P(('seq', 'grp')), may hold values from -64 to 64
- keys: bfloat16 [65536, 1024], P(('seq', 'grp')), may hold values from -4.5 to 4.5
- values: bfloat16 [65536, 1024], P(('seq', 'grp')), may hold values from -4.5 to 4.5
- output_cotangent: bfloat16 [65536, 4096], P(('seq', 'grp')), may hold values from -4.5 to 4.5
- select: int32 [512, 8, 8], P(None, 'grp'), may hold values from 0 to 511, as said below
Outputs:
- grad_query: bfloat16 [65536, 4096], P('seq', 'grp')
- key_gradient: bfloat16 [65536, 1024], P('seq', 'grp')
- value_gradient: bfloat16 [65536, 1024], P('seq', 'grp')
The draws below stay inside these ranges and needn't reach their ends.
Inputs may be any that keep to these rules, and one draw needn't show every extreme that they name: select[b, c, 0] = b; the other 7 entries of a row are distinct blocks other than b, all earlier than b when b >= 7; for smaller b they are the b earlier blocks and some later ones.
All inputs are finite; a program needn't handle non-finite values.
Results may differ from the reference program's by a relative error of at most 0.019.
Values may be sent and summed in bfloat16 or wider, within the bound.
A program may use at most 128 MiB of HBM per device.

```python
import jax
import jax.numpy as jnp
from jax import lax

HEAD_SIZE = 128
QUERY_HEADS = 32
KEY_HEADS = 8
BLOCK_TOKENS = 128
CHOSEN_BLOCKS = 8
SEQUENCE_LENGTH = 65536
SEQUENCE_BLOCKS = 512


def key_table(key):
    return jnp.clip(jax.random.normal(key, (SEQUENCE_LENGTH, KEY_HEADS * HEAD_SIZE), jnp.float32), -4.5, 4.5)


def draw_keys(key, part):
    random_base_keys = key_table(key)
    return random_base_keys.astype(jnp.bfloat16)


def draw_query(key, part):
    key = jax.random.fold_in(key, 12)
    draws_raw = jnp.clip(jax.random.normal(key, (SEQUENCE_LENGTH, QUERY_HEADS * HEAD_SIZE), jnp.float32), -4.5, 4.5)
    return draws_raw.astype(jnp.bfloat16)


def draw_select(key, part):
    key = jax.random.fold_in(key, 13)
    score_matrix = jax.random.randint(key, (SEQUENCE_BLOCKS, KEY_HEADS, SEQUENCE_BLOCKS), 0, 65536)
    blocks = jnp.arange(SEQUENCE_BLOCKS, dtype=jnp.int32)
    diagonal_block = blocks[:, None, None]
    ranking = score_matrix * SEQUENCE_BLOCKS + blocks[None, None, :]
    earlier = blocks[None, None, :] < diagonal_block
    after_own = blocks[None, None, :] > diagonal_block
    ranking = jnp.where(earlier, ranking + 536870912, jnp.where(after_own, ranking, -1))
    dummy, picked = lax.top_k(ranking, CHOSEN_BLOCKS - 1)
    leading_column = jnp.broadcast_to(diagonal_block, (SEQUENCE_BLOCKS, KEY_HEADS, 1))
    return jnp.concatenate([leading_column, picked.astype(jnp.int32)], axis=2).astype(jnp.int32)


def level_of(rng, dims, split, smallest, largest):
    def one(dim, shards_of):
        heights = jax.random.uniform(jax.random.fold_in(jax.random.fold_in(rng, 6), dim), (shards_of,), jnp.float32, smallest / len(split), largest / len(split))
        return jnp.repeat(jnp.exp(heights), dims[dim] // shards_of).reshape((-1,) + (1,) * (len(dims) - dim - 1))

    level = one(*split[0])
    for cut in split[1:]:
        level = level * one(*cut)
    return level


def centred(own_key, dims, deviation, bound, shards=(), kind=jnp.bfloat16):
    values = deviation * jax.random.normal(own_key, dims, jnp.float32)
    if shards:
        values = values * level_of(own_key, dims, shards, -0.22, 0.18)
    return jnp.clip(values, -bound, bound).astype(kind)


def setup_inputs(seed: int = 0) -> dict:
    arg_keys = jax.random.split(jax.random.key(seed), 6)
    return {
        "query": draw_query(jax.random.fold_in(arg_keys[5], 71), 0),
        "keys": draw_keys(jax.random.fold_in(arg_keys[5], 71), 0),
        "values": centred(arg_keys[2], (SEQUENCE_LENGTH, KEY_HEADS * HEAD_SIZE), 1.0, 4.5, ((0, 512),)),
        "output_cotangent": centred(arg_keys[3], (SEQUENCE_LENGTH, QUERY_HEADS * HEAD_SIZE), 1.0, 4.5, ((0, 512),)),
        "select": draw_select(jax.random.fold_in(arg_keys[5], 71), 0),
    }


def product(pattern, first_op, second_op):
    return jnp.einsum(pattern, first_op.astype(jnp.float32), second_op.astype(jnp.float32))


def block_backward(q_rows, grad_rows, key_value_pairs, query_pos, key_positions, factor):
    head_width = q_rows.shape[-1]
    keys_part = key_value_pairs[..., :head_width]
    vals_part = key_value_pairs[..., head_width:]
    score_matrix = product("tcgd,ckd->cgtk", q_rows, keys_part) * factor
    allowed = key_positions[:, None, None, :] <= query_pos[None, None, :, None]
    score_matrix = jnp.where(allowed, score_matrix, -jnp.inf)
    highest = jnp.max(score_matrix, axis=3, keepdims=True)
    weights = jnp.exp(score_matrix - highest)
    probability = weights / jnp.sum(weights, axis=3, keepdims=True)
    probs_low = lax.optimization_barrier(probability.astype(jnp.bfloat16))
    recomputed = product("cgtk,ckd->tcgd", probs_low, vals_part)
    row_delta = jnp.sum(grad_rows.astype(jnp.float32) * recomputed, axis=3)
    row_delta = jnp.transpose(row_delta, (1, 2, 0))[..., None]
    dprobs = product("tcgd,ckd->cgtk", grad_rows, vals_part)
    dscores = lax.optimization_barrier((probability * (dprobs - row_delta)).astype(jnp.bfloat16))
    grad_q = product("cgtk,ckd->tcgd", dscores, keys_part) * factor
    grad_k = product("cgtk,tcgd->ckd", dscores, q_rows) * factor
    grad_v = product("cgtk,tcgd->ckd", probs_low, grad_rows)
    return grad_q, jnp.concatenate([grad_k, grad_v], axis=-1)


def reference(query, keys, values, output_cotangent, select):
    query_group_size = QUERY_HEADS // KEY_HEADS
    factor = HEAD_SIZE ** -0.5
    block_count = select.shape[0]
    query_full = query.reshape(block_count, BLOCK_TOKENS, KEY_HEADS, query_group_size, HEAD_SIZE)
    output_gradient_full = output_cotangent.reshape(block_count, BLOCK_TOKENS, KEY_HEADS, query_group_size, HEAD_SIZE)
    key_value_pairs = jnp.concatenate([keys.reshape(block_count, BLOCK_TOKENS, KEY_HEADS, HEAD_SIZE), values.reshape(block_count, BLOCK_TOKENS, KEY_HEADS, HEAD_SIZE)], axis=3)
    head_numbers = jnp.arange(KEY_HEADS, dtype=jnp.int32)[:, None]
    block_offsets = jnp.arange(BLOCK_TOKENS, dtype=jnp.int32)

    def advance(total_sums, block_index):
        chosen_indices = select[block_index]
        gathered_rows = key_value_pairs[chosen_indices, :, head_numbers, :].reshape(KEY_HEADS, CHOSEN_BLOCKS * BLOCK_TOKENS, 2 * HEAD_SIZE)
        key_positions = (chosen_indices[:, :, None] * BLOCK_TOKENS + block_offsets).reshape(KEY_HEADS, CHOSEN_BLOCKS * BLOCK_TOKENS)
        query_pos = block_index * BLOCK_TOKENS + block_offsets
        grad_q, key_value_gradient = block_backward(query_full[block_index], output_gradient_full[block_index], gathered_rows, query_pos, key_positions, factor)
        total_sums = total_sums.at[chosen_indices, :, head_numbers, :].add(key_value_gradient.reshape(KEY_HEADS, CHOSEN_BLOCKS, BLOCK_TOKENS, 2 * HEAD_SIZE))
        return total_sums, grad_q.astype(jnp.bfloat16)

    initial_state = jnp.zeros((block_count, BLOCK_TOKENS, KEY_HEADS, 2 * HEAD_SIZE), jnp.float32)
    total_sums, query_grads = lax.scan(advance, initial_state, jnp.arange(block_count, dtype=jnp.int32))
    grad_query = query_grads.reshape(block_count * BLOCK_TOKENS, QUERY_HEADS * HEAD_SIZE)
    key_gradient = total_sums[..., :HEAD_SIZE].astype(jnp.bfloat16).reshape(block_count * BLOCK_TOKENS, KEY_HEADS * HEAD_SIZE)
    value_gradient = total_sums[..., HEAD_SIZE:].astype(jnp.bfloat16).reshape(block_count * BLOCK_TOKENS, KEY_HEADS * HEAD_SIZE)
    return grad_query, key_gradient, value_gradient
```

```python
import functools

import jax
import jax.numpy as jnp
from jax import lax
from jax.experimental import pallas as pl
from jax.experimental.pallas import tpu as pltpu
from jax.sharding import PartitionSpec as P

HEAD_SIZE = 128
QUERY_HEADS = 32
KEY_HEADS = 8
BLOCK_TOKENS = 128
CHOSEN_BLOCKS = 8
GROUP = QUERY_HEADS // KEY_HEADS
PAIR = 2 * HEAD_SIZE
STRIPES = 8
ROWS = BLOCK_TOKENS // STRIPES
KEYS = CHOSEN_BLOCKS * BLOCK_TOKENS
FACTOR = HEAD_SIZE ** (-0.5)
VMEM = 56 * 1024 * 1024


def pack_kernel(sel, table, out):
    @pl.loop(0, sel.shape[0], unroll=8)
    def _(r):
        out[r] = table[sel[r]]


def accumulate_kernel(sel, rows, out, total):
    total[...] = jnp.zeros_like(total)

    @pl.loop(0, sel.shape[0], unroll=8)
    def _(r):
        total[sel[r]] += rows[r].astype(jnp.float32)

    out[...] = total[...].astype(out.dtype)


def nt(a, b):
    return lax.dot_general(a, b, (((1,), (1,)), ((), ())), preferred_element_type=jnp.float32)


def nn(a, b):
    return jnp.dot(a, b, preferred_element_type=jnp.float32)


def attention_kernel(sel, q_ref, g_ref, kv_ref, dq_ref, dkv_ref, probs, dscores):
    step = pl.program_id(0)
    keys = kv_ref[:, 0, :, :, :HEAD_SIZE].reshape(KEYS, HEAD_SIZE)
    vals = kv_ref[:, 0, :, :, HEAD_SIZE:].reshape(KEYS, HEAD_SIZE)
    stripe = lax.broadcasted_iota(jnp.int32, (STRIPES, ROWS, BLOCK_TOKENS), 0)
    row = lax.broadcasted_iota(jnp.int32, (STRIPES, ROWS, BLOCK_TOKENS), 1)
    token = lax.broadcasted_iota(jnp.int32, (STRIPES, ROWS, BLOCK_TOKENS), 2)
    ahead = stripe * ROWS + row - token
    own = sel[step * CHOSEN_BLOCKS]
    bias = jnp.stack(
        [
            jnp.where(
                ahead <= (own - sel[step * CHOSEN_BLOCKS + j]) * BLOCK_TOKENS, 0.0, -jnp.inf
            ).astype(jnp.float32)
            for j in range(CHOSEN_BLOCKS)
        ],
        axis=1,
    ).reshape(KEYS, BLOCK_TOKENS)
    for h in range(GROUP):
        cols = pl.ds(h * HEAD_SIZE, HEAD_SIZE)
        q, g = q_ref[:, cols], g_ref[:, cols]
        scores = nt(keys, q) * FACTOR + bias
        highest = jnp.max(scores, axis=0, keepdims=True)
        weights = jnp.exp(scores - highest)
        prob = weights * (1.0 / jnp.sum(weights, axis=0, keepdims=True))
        low = prob.astype(jnp.bfloat16)
        dprobs = nt(vals, g)
        delta = jnp.sum(low.astype(jnp.float32) * dprobs, axis=0, keepdims=True)
        probs[:, cols] = low
        dscores[:, cols] = (prob * (dprobs - delta)).astype(jnp.bfloat16)
    q_rows = jnp.concatenate([q_ref[:, h * HEAD_SIZE : (h + 1) * HEAD_SIZE] for h in range(GROUP)], 0)
    g_rows = jnp.concatenate([g_ref[:, h * HEAD_SIZE : (h + 1) * HEAD_SIZE] for h in range(GROUP)], 0)
    dk = nn(dscores[...], q_rows) * FACTOR
    dv = nn(probs[...], g_rows)
    full = (STRIPES, CHOSEN_BLOCKS, ROWS, HEAD_SIZE)
    dkv_ref[:, 0, :, :, :HEAD_SIZE] = dk.astype(jnp.bfloat16).reshape(full)
    dkv_ref[:, 0, :, :, HEAD_SIZE:] = dv.astype(jnp.bfloat16).reshape(full)
    dq_t = nn(keys.T, dscores[...]) * FACTOR
    for h in range(GROUP):
        cols = pl.ds(h * HEAD_SIZE, HEAD_SIZE)
        dq_ref[:, cols] = dq_t[:, h * HEAD_SIZE : (h + 1) * HEAD_SIZE].T.astype(jnp.bfloat16)


def pack(sel, table):
    return pl.pallas_call(
        pack_kernel,
        out_shape=jax.ShapeDtypeStruct((sel.shape[0],) + table.shape[1:], table.dtype),
        in_specs=[
            pl.BlockSpec(memory_space=pltpu.SMEM),
            pl.BlockSpec(memory_space=pltpu.VMEM),
        ],
        out_specs=pl.BlockSpec(memory_space=pltpu.VMEM),
        compiler_params=pltpu.CompilerParams(vmem_limit_bytes=VMEM),
        name="pack",
    )(sel, table)


def accumulate(sel, rows, blocks):
    return pl.pallas_call(
        accumulate_kernel,
        out_shape=jax.ShapeDtypeStruct((blocks,) + rows.shape[1:], rows.dtype),
        in_specs=[
            pl.BlockSpec(memory_space=pltpu.SMEM),
            pl.BlockSpec(memory_space=pltpu.VMEM),
        ],
        out_specs=pl.BlockSpec(memory_space=pltpu.VMEM),
        scratch_shapes=[pltpu.VMEM((blocks,) + rows.shape[1:], jnp.float32)],
        compiler_params=pltpu.CompilerParams(vmem_limit_bytes=VMEM),
        name="accumulate",
    )(sel, rows)


def attention(sel, q, g, kv):
    steps = kv.shape[1]
    rows = pl.BlockSpec((BLOCK_TOKENS, GROUP * HEAD_SIZE), lambda i, s: (i, 0))
    pairs = pl.BlockSpec((STRIPES, 1, CHOSEN_BLOCKS, ROWS, PAIR), lambda i, s: (0, i, 0, 0, 0))
    return pl.pallas_call(
        attention_kernel,
        out_shape=(
            jax.ShapeDtypeStruct(q.shape, jnp.bfloat16),
            jax.ShapeDtypeStruct(kv.shape, jnp.bfloat16),
        ),
        grid_spec=pltpu.PrefetchScalarGridSpec(
            num_scalar_prefetch=1,
            grid=(steps,),
            in_specs=[rows, rows, pairs],
            out_specs=[rows, pairs],
            scratch_shapes=[pltpu.VMEM((KEYS, GROUP * BLOCK_TOKENS), jnp.bfloat16)] * 2,
        ),
        compiler_params=pltpu.CompilerParams(vmem_limit_bytes=VMEM),
        name="attention",
    )(sel, q, g, kv)


def body(query, keys, values, output_cotangent, select):
    qblocks = lax.axis_size("grp")
    columns = lax.axis_size("xc")
    row_blocks = columns * qblocks
    blocks = select.shape[0]
    row = lax.axis_index("y")
    column = lax.axis_index("xc")
    flat = select.reshape(blocks * CHOSEN_BLOCKS)
    width = row_blocks * CHOSEN_BLOCKS
    row_select = lax.dynamic_slice_in_dim(flat, row * width, width, 0)
    own_select = lax.dynamic_slice_in_dim(
        flat, row * width + column * qblocks * CHOSEN_BLOCKS, qblocks * CHOSEN_BLOCKS, 0
    )
    pairs = jnp.concatenate(
        [
            keys.reshape(columns, ROWS, KEY_HEADS, HEAD_SIZE),
            values.reshape(columns, ROWS, KEY_HEADS, HEAD_SIZE),
        ],
        axis=3,
    )
    pairs = jnp.transpose(pairs, (0, 2, 1, 3)).reshape(columns * KEY_HEADS, ROWS, PAIR)
    share = lax.all_to_all(pairs, ("xc", "grp"), split_axis=0, concat_axis=0, tiled=True)
    table = lax.all_gather(share, "y", axis=0, tiled=True)
    q_heads = lax.all_to_all(query, "grp", split_axis=1, concat_axis=0, tiled=True)
    g_heads = lax.all_to_all(output_cotangent, "grp", split_axis=1, concat_axis=0, tiled=True)
    outgoing = pack(row_select, table)
    incoming = lax.all_to_all(outgoing, "xc", split_axis=0, concat_axis=0, tiled=True)
    incoming = incoming.reshape(columns, qblocks, CHOSEN_BLOCKS, ROWS, PAIR)
    grad_query, unit_grads = attention(own_select, q_heads, g_heads, incoming)
    returned = lax.all_to_all(
        unit_grads.reshape(width, ROWS, PAIR), "xc", split_axis=0, concat_axis=0, tiled=True
    )
    sums = accumulate(row_select, returned, blocks)
    row_sums = lax.psum_scatter(sums, "y", scatter_dimension=0, tiled=True)
    own = lax.all_to_all(row_sums, "xc", split_axis=0, concat_axis=0, tiled=True)
    own = jnp.transpose(own.reshape(columns, qblocks, ROWS, PAIR), (1, 0, 2, 3))
    own = own.reshape(qblocks * BLOCK_TOKENS, PAIR)
    return grad_query, own[:, :HEAD_SIZE], own[:, HEAD_SIZE:]


def solution(mesh):
    groups = mesh.shape["grp"]
    grid = jax.sharding.Mesh(
        mesh.devices.reshape(-1, STRIPES, groups), ("y", "xc", "grp")
    )
    rows = ("y", "xc")
    in_specs = (P(rows + ("grp",), None),) * 4 + (P(None, "grp", None),)
    out_specs = (P(rows, "grp"),) * 3
    return jax.shard_map(
        body, mesh=grid, in_specs=in_specs, out_specs=out_specs, check_vma=False
    )
```

```python
import functools

import jax
import jax.numpy as jnp
from jax import lax
from jax.experimental import pallas as pl
from jax.experimental.pallas import tpu as pltpu
from jax.sharding import PartitionSpec as P

HEAD_SIZE = 128
QUERY_HEADS = 32
KEY_HEADS = 8
BLOCK_TOKENS = 128
CHOSEN_BLOCKS = 8
GROUP = QUERY_HEADS // KEY_HEADS
PAIR = 2 * HEAD_SIZE
STRIPES = 8
ROWS = BLOCK_TOKENS // STRIPES
KEYS = CHOSEN_BLOCKS * BLOCK_TOKENS
FACTOR = HEAD_SIZE ** (-0.5)
VMEM = 56 * 1024 * 1024


def accumulate_kernel(sel, k_rows, v_rows, out, total):
    total[...] = jnp.zeros_like(total)

    @pl.loop(0, sel.shape[0], unroll=8)
    def _(r):
        total[sel[r], :, :HEAD_SIZE] += k_rows[r].astype(jnp.float32)
        total[sel[r], :, HEAD_SIZE:] += v_rows[r].astype(jnp.float32)

    out[...] = total[...].astype(out.dtype)


def nt(a, b):
    return lax.dot_general(a, b, (((1,), (1,)), ((), ())), preferred_element_type=jnp.float32)


def nn(a, b):
    return jnp.dot(a, b, preferred_element_type=jnp.float32)


def attention_block(i, own, sel_at, q_ref, g_ref, k_ref, v_ref, dq_ref, dk_ref, dv_ref, probs, dscores):
    rows = pl.ds(pl.multiple_of(i * BLOCK_TOKENS, BLOCK_TOKENS), BLOCK_TOKENS)
    units = pl.ds(pl.multiple_of(i * CHOSEN_BLOCKS, CHOSEN_BLOCKS), CHOSEN_BLOCKS)
    keys = k_ref[:, units].reshape(KEYS, HEAD_SIZE)
    vals = v_ref[:, units].reshape(KEYS, HEAD_SIZE)
    stripe = lax.broadcasted_iota(jnp.int32, (STRIPES, ROWS, BLOCK_TOKENS), 0)
    row = lax.broadcasted_iota(jnp.int32, (STRIPES, ROWS, BLOCK_TOKENS), 1)
    token = lax.broadcasted_iota(jnp.int32, (STRIPES, ROWS, BLOCK_TOKENS), 2)
    ahead = stripe * ROWS + row - token
    bias = jnp.stack(
        [
            jnp.where(ahead <= (own - sel_at(j)) * BLOCK_TOKENS, 0.0, -jnp.inf).astype(jnp.float32)
            for j in range(CHOSEN_BLOCKS)
        ],
        axis=1,
    ).reshape(KEYS, BLOCK_TOKENS)
    q_parts, g_parts = [], []
    for h in range(GROUP):
        cols = pl.ds(h * HEAD_SIZE, HEAD_SIZE)
        q, g = q_ref[i, :, cols], g_ref[i, :, cols]
        q_parts.append(q)
        g_parts.append(g)
        scores = nt(keys, q) * FACTOR + bias
        highest = jnp.max(scores, axis=0, keepdims=True)
        weights = jnp.exp(scores - highest)
        prob = weights * (1.0 / jnp.sum(weights, axis=0, keepdims=True))
        low = prob.astype(jnp.bfloat16)
        dprobs = nt(vals, g)
        delta = jnp.sum(low.astype(jnp.float32) * dprobs, axis=0, keepdims=True)
        probs[:, cols] = low
        dscores[:, cols] = (prob * (dprobs - delta)).astype(jnp.bfloat16)
    full = (STRIPES, CHOSEN_BLOCKS, ROWS, HEAD_SIZE)
    dv = nn(probs[...], jnp.concatenate(g_parts, 0))
    dv_ref[:, units] = dv.astype(jnp.bfloat16).reshape(full)
    dk = nn(dscores[...], jnp.concatenate(q_parts, 0)) * FACTOR
    dk_ref[:, units] = dk.astype(jnp.bfloat16).reshape(full)
    dq_t = nn(keys.T, dscores[...]) * FACTOR
    for h in range(GROUP):
        cols = pl.ds(h * HEAD_SIZE, HEAD_SIZE)
        dq_ref[rows, cols] = dq_t[:, h * HEAD_SIZE : (h + 1) * HEAD_SIZE].T.astype(jnp.bfloat16)


Y, C, Z = 8, 8, 8
UNITS = Z * CHOSEN_BLOCKS
SHARE = C * Z
HALF = SHARE // 2
STEPS = 4
SPLITS = 4
WIDE = GROUP * HEAD_SIZE


def at(index, size):
    return pl.ds(pl.multiple_of(index * size, size), size)


def front_kernel(
    sel, k, v, q, g, dq, ret_k_out, ret_v_out,
    kz, vz, qh, gh, tab_k, tab_v, out_k, out_v, in_k, in_v, dk_out, dv_out, ret_k, ret_v, probs, dscores,
    z_send, z_recv, s_send, s_recv, ag_send, ag_recv, k_send, k_recv, v_send, v_recv,
    rv_send, rv_recv, rk_send, rk_recv, own_sem,
):
    y, c, z = lax.axis_index("y"), lax.axis_index("xc"), lax.axis_index("grp")

    def device(dy=0, dc=0, dz=0):
        return (lax.rem(y + dy + Y, Y), lax.rem(c + dc, C), lax.rem(z + dz, Z))

    def remote(src, dst, send, recv, target):
        return pltpu.make_async_remote_copy(
            src_ref=src, dst_ref=dst, send_sem=send, recv_sem=recv,
            device_id=target, device_id_type=pl.DeviceIdType.MESH,
        )

    barrier = pltpu.get_barrier_semaphore()
    partners = [device(dz=d) for d in range(1, Z)] + [device(dc=d) for d in range(1, C)]
    partners += [device(dy=1), device(dy=-1)]
    for p in partners:
        pl.semaphore_signal(barrier, inc=1, device_id=p, device_id_type=pl.DeviceIdType.MESH)
    pl.semaphore_wait(barrier, len(partners))

    def z_copy(n, src, width, dst, d):
        to = lax.rem(z + d, Z)
        return remote(src.at[:, at(to, width)], dst.at[z], z_send.at[n, d], z_recv.at[n, d], device(dz=d))

    for d in range(1, Z):
        z_copy(0, k, HEAD_SIZE, kz, d).start()
        z_copy(1, v, HEAD_SIZE, vz, d).start()
    kz[z] = k[:, at(z, HEAD_SIZE)]
    vz[z] = v[:, at(z, HEAD_SIZE)]
    for d in range(1, Z):
        z_copy(0, k, HEAD_SIZE, kz, d).wait_recv()
        z_copy(1, v, HEAD_SIZE, vz, d).wait_recv()

    mine = pl.ds(pl.multiple_of(y * SHARE + c * Z, Z), Z)

    def s_copy(n, src, tab, d):
        to = lax.rem(c + d, C)
        return remote(src.at[:, at(to, ROWS)], tab.at[mine], s_send.at[n, d], s_recv.at[n, d], device(dc=d))

    for d in range(1, C):
        s_copy(0, kz, tab_k, d).start()
        s_copy(1, vz, tab_v, d).start()
    for d in range(1, Z):
        z_copy(2, q, WIDE, qh, d).start()
        z_copy(3, g, WIDE, gh, d).start()
    tab_k[mine] = kz[:, at(c, ROWS)]
    tab_v[mine] = vz[:, at(c, ROWS)]
    qh[z] = q[:, at(z, WIDE)]
    gh[z] = g[:, at(z, WIDE)]

    def ring(n, tab, s, way, half):
        owner = lax.rem(y - way * s + Y, Y)
        part = tab.at[pl.ds(pl.multiple_of(owner * SHARE + half * HALF, HALF), HALF)]
        lane = 0 if way > 0 else 1
        return remote(part, part, ag_send.at[n, s, lane, half], ag_recv.at[n, s, lane, half], device(dy=way))

    order = ((1, 0), (-1, 1), (1, 1), (-1, 0))

    def ring_first(n, tab):
        for way, half in order:
            ring(n, tab, 0, way, half).start()

    def ring_next(n, tab, s):
        for way, half in order[: 2 if s == STEPS - 1 else 4]:
            ring(n, tab, s - 1, way, half).wait_recv()
            ring(n, tab, s, way, half).start()

    def ring_last(n, tab):
        for way, half in order[2:]:
            ring(n, tab, STEPS - 2, way, half).wait_recv()
        for way, half in order[:2]:
            ring(n, tab, STEPS - 1, way, half).wait_recv()

    def pack(tab, out, own, first, count):
        for d in range(C):
            to = lax.rem(c + d, C)

            @pl.loop(0, count, unroll=8)
            def _(u):
                rows = tab[sel[to * UNITS + first + u]]
                if d:
                    out[d, first + u] = rows
                else:
                    own[c, first + u] = rows

    def k_copy(d):
        return remote(out_k.at[d], in_k.at[c], k_send.at[d], k_recv.at[d], device(dc=d))

    part = UNITS // SPLITS

    def v_copy(d, n):
        return remote(
            out_v.at[d, at(n, part)], in_v.at[c, at(n, part)], v_send.at[d, n], v_recv.at[d, n], device(dc=d)
        )

    def rv_copy(d, n):
        to = lax.rem(c + d, C)
        return remote(
            dv_out.at[to, at(n, part)], ret_v.at[c, at(n, part)], rv_send.at[d, n], rv_recv.at[d, n], device(dc=d)
        )

    def rk_copy(d):
        to = lax.rem(c + d, C)
        return remote(dk_out.at[to], ret_k.at[c], rk_send.at[d], rk_recv.at[d], device(dc=d))

    for d in range(1, C):
        s_copy(0, kz, tab_k, d).wait_recv()
    ring_first(0, tab_k)
    for d in range(1, C):
        s_copy(1, vz, tab_v, d).wait_recv()
    for s in range(1, STEPS):
        ring_next(0, tab_k, s)
    ring_first(1, tab_v)
    ring_last(0, tab_k)
    pack(tab_k, out_k, in_k, 0, UNITS)
    for d in range(1, C):
        k_copy(d).start()
    for s in range(1, STEPS):
        ring_next(1, tab_v, s)
    ring_last(1, tab_v)

    for n in range(SPLITS):
        pack(tab_v, out_v, in_v, n * part, part)
        for d in range(1, C):
            v_copy(d, n).start()

    for d in range(1, Z):
        z_copy(2, q, WIDE, qh, d).wait_recv()
        z_copy(3, g, WIDE, gh, d).wait_recv()
    for d in range(1, C):
        k_copy(d).wait_recv()

    @pl.loop(0, SPLITS)
    def _(n):
        for d in range(1, C):
            v_copy(d, n).wait_recv()

        @pl.loop(0, Z // SPLITS)
        def _(m):
            i = n * (Z // SPLITS) + m
            first = c * UNITS + i * CHOSEN_BLOCKS
            attention_block(
                i, sel[first], lambda j: sel[first + j],
                qh, gh, in_k, in_v, dq, dk_out, dv_out, probs, dscores,
            )

        for d in range(1, C):
            rv_copy(d, n).start()

    for d in range(1, C):
        rk_copy(d).start()
    own_v = pltpu.make_async_copy(dv_out.at[c], ret_v.at[c], own_sem.at[0])
    own_k = pltpu.make_async_copy(dk_out.at[c], ret_k.at[c], own_sem.at[1])
    own_v.start()
    own_k.start()
    own_v.wait()
    own_k.wait()
    for d in range(1, C):
        for n in range(SPLITS):
            rv_copy(d, n).wait_recv()
    for d in range(1, C):
        rk_copy(d).wait_recv()
    ret_k_out[...] = ret_k[...]
    ret_v_out[...] = ret_v[...]

    for d in range(1, Z):
        for n, (src, width, dst) in enumerate(
            ((k, HEAD_SIZE, kz), (v, HEAD_SIZE, vz), (q, WIDE, qh), (g, WIDE, gh))
        ):
            z_copy(n, src, width, dst, d).wait_send()
    for d in range(1, C):
        s_copy(0, kz, tab_k, d).wait_send()
        s_copy(1, vz, tab_v, d).wait_send()
        k_copy(d).wait_send()
        rk_copy(d).wait_send()
        for n in range(SPLITS):
            v_copy(d, n).wait_send()
            rv_copy(d, n).wait_send()
    for n, tab in ((0, tab_k), (1, tab_v)):
        for s in range(STEPS):
            for way, half in order[: 2 if s == STEPS - 1 else 4]:
                ring(n, tab, s, way, half).wait_send()


def front(sel, k, v, q, g):
    vmem = pl.BlockSpec(memory_space=pltpu.VMEM)
    bf16 = lambda *shape: pltpu.VMEM(shape, jnp.bfloat16)
    dma = lambda *shape: pltpu.SemaphoreType.DMA(shape)
    units = (C, UNITS, ROWS, HEAD_SIZE)
    table = (Y * SHARE, ROWS, HEAD_SIZE)
    return pl.pallas_call(
        front_kernel,
        out_shape=(
            jax.ShapeDtypeStruct((Z * BLOCK_TOKENS, WIDE), jnp.bfloat16),
            jax.ShapeDtypeStruct(units, jnp.bfloat16),
            jax.ShapeDtypeStruct(units, jnp.bfloat16),
        ),
        in_specs=[pl.BlockSpec(memory_space=pltpu.SMEM)] + [vmem] * 4,
        out_specs=[vmem] * 3,
        scratch_shapes=[bf16(Z, BLOCK_TOKENS, HEAD_SIZE)] * 2
        + [bf16(Z, BLOCK_TOKENS, WIDE)] * 2
        + [bf16(*table)] * 2
        + [bf16(*units)] * 8
        + [bf16(KEYS, WIDE)] * 2
        + [dma(4, Z)] * 2
        + [dma(2, C)] * 2
        + [dma(2, STEPS, 2, 2)] * 2
        + [dma(C)] * 2
        + [dma(C, SPLITS)] * 2
        + [dma(C, SPLITS)] * 2
        + [dma(C)] * 2
        + [dma(2)],
        compiler_params=pltpu.CompilerParams(
            vmem_limit_bytes=VMEM, collective_id=0, has_side_effects=True
        ),
        name="front",
    )(sel, k, v, q, g)


def accumulate(sel, k_rows, v_rows, blocks):
    shape = (blocks, ROWS, PAIR)
    return pl.pallas_call(
        accumulate_kernel,
        out_shape=jax.ShapeDtypeStruct(shape, jnp.bfloat16),
        in_specs=[
            pl.BlockSpec(memory_space=pltpu.SMEM),
            pl.BlockSpec(memory_space=pltpu.VMEM),
            pl.BlockSpec(memory_space=pltpu.VMEM),
        ],
        out_specs=pl.BlockSpec(memory_space=pltpu.VMEM),
        scratch_shapes=[pltpu.VMEM(shape, jnp.float32)],
        compiler_params=pltpu.CompilerParams(vmem_limit_bytes=VMEM),
        name="accumulate",
    )(sel, k_rows, v_rows)


def body(query, keys, values, output_cotangent, select):
    row = lax.axis_index("y")
    flat = select.reshape(Y * SHARE * CHOSEN_BLOCKS)
    width = C * UNITS
    row_select = lax.dynamic_slice_in_dim(flat, row * width, width, 0)
    grad_query, ret_k, ret_v = front(row_select, keys, values, query, output_cotangent)
    rows = (width, ROWS, HEAD_SIZE)
    sums = accumulate(row_select, ret_k.reshape(rows), ret_v.reshape(rows), Y * SHARE)
    row_sums = lax.psum_scatter(sums, "y", scatter_dimension=0, tiled=True)
    own = lax.all_to_all(row_sums, "xc", split_axis=0, concat_axis=0, tiled=True)
    own = jnp.transpose(own.reshape(C, Z, ROWS, PAIR), (1, 0, 2, 3))
    own = own.reshape(Z * BLOCK_TOKENS, PAIR)
    return grad_query, own[:, :HEAD_SIZE], own[:, HEAD_SIZE:]


def solution(mesh):
    groups = mesh.shape["grp"]
    grid = jax.sharding.Mesh(
        mesh.devices.reshape(-1, STRIPES, groups), ("y", "xc", "grp")
    )
    rows = ("y", "xc")
    in_specs = (P(rows + ("grp",), None),) * 4 + (P(None, "grp", None),)
    out_specs = (P(rows, "grp"),) * 3
    return jax.shard_map(
        body, mesh=grid, in_specs=in_specs, out_specs=out_specs, check_vma=False
    )
```

```python
import functools

import jax
import jax.numpy as jnp
from jax import lax
from jax.experimental import pallas as pl
from jax.experimental.pallas import tpu as pltpu
from jax.sharding import PartitionSpec as P

HEAD_SIZE = 128
QUERY_HEADS = 32
KEY_HEADS = 8
BLOCK_TOKENS = 128
CHOSEN_BLOCKS = 8
GROUP = QUERY_HEADS // KEY_HEADS
STRIPES = 8
ROWS = BLOCK_TOKENS // STRIPES
KEYS = CHOSEN_BLOCKS * BLOCK_TOKENS
FACTOR = HEAD_SIZE ** (-0.5)
VMEM = 56 * 1024 * 1024


def nt(a, b):
    return lax.dot_general(a, b, (((1,), (1,)), ((), ())), preferred_element_type=jnp.float32)


def nn(a, b):
    return jnp.dot(a, b, preferred_element_type=jnp.float32)


Y, C, Z = 8, 8, 8
OTHERS = CHOSEN_BLOCKS - 1
OTHER_KEYS = OTHERS * BLOCK_TOKENS
UNITS = Z * OTHERS
REQUESTS = C * UNITS
SLOTS = C * Z * CHOSEN_BLOCKS
SHARE = C * Z
BLOCKS = Y * SHARE
HALF = SHARE // 2
STEPS = 4
SPLITS = 4
PER_SPLIT = Z // SPLITS
WIDE = GROUP * HEAD_SIZE


def at(index, size):
    return pl.ds(pl.multiple_of(index * size, size), size)


def attention_block(
    i, own, sel_at, q_ref, g_ref, kz, vz, k_ref, v_ref, dq_ref, dk_own, dv_own, dk_ref, dv_ref, probs, dscores
):
    units = pl.ds(i * OTHERS, OTHERS)
    keys = jnp.concatenate([kz[i], k_ref[:, units].reshape(OTHER_KEYS, HEAD_SIZE)], 0)
    vals = jnp.concatenate([vz[i], v_ref[:, units].reshape(OTHER_KEYS, HEAD_SIZE)], 0)
    row = lax.broadcasted_iota(jnp.int32, (BLOCK_TOKENS, BLOCK_TOKENS), 0)
    token = lax.broadcasted_iota(jnp.int32, (BLOCK_TOKENS, BLOCK_TOKENS), 1)
    own_bias = jnp.where(row <= token, 0.0, -jnp.inf).astype(jnp.float32)
    other_bias = jnp.stack(
        [
            jnp.full(
                (STRIPES, ROWS, BLOCK_TOKENS), jnp.where(sel_at(j) < own, 0.0, -jnp.inf), jnp.float32
            )
            for j in range(1, CHOSEN_BLOCKS)
        ],
        axis=1,
    ).reshape(OTHER_KEYS, BLOCK_TOKENS)
    bias = jnp.concatenate([own_bias, other_bias], 0)
    q_parts, g_parts = [], []
    for h in range(GROUP):
        cols = pl.ds(h * HEAD_SIZE, HEAD_SIZE)
        q, g = q_ref[i, :, cols], g_ref[i, :, cols]
        q_parts.append(q)
        g_parts.append(g)
        scores = nt(keys, q) * FACTOR + bias
        highest = jnp.max(scores, axis=0, keepdims=True)
        weights = jnp.exp(scores - highest)
        prob = weights * (1.0 / jnp.sum(weights, axis=0, keepdims=True))
        low = prob.astype(jnp.bfloat16)
        dprobs = nt(vals, g)
        delta = jnp.sum(low.astype(jnp.float32) * dprobs, axis=0, keepdims=True)
        probs[:, cols] = low
        dscores[:, cols] = (prob * (dprobs - delta)).astype(jnp.bfloat16)
    others = (STRIPES, OTHERS, ROWS, HEAD_SIZE)
    dv = nn(probs[...], jnp.concatenate(g_parts, 0))
    dv_own[i] = dv[:BLOCK_TOKENS]
    dv_ref[:, units] = dv[BLOCK_TOKENS:].astype(jnp.bfloat16).reshape(others)
    dk = nn(dscores[...], jnp.concatenate(q_parts, 0)) * FACTOR
    dk_own[i] = dk[:BLOCK_TOKENS]
    dk_ref[:, units] = dk[BLOCK_TOKENS:].astype(jnp.bfloat16).reshape(others)
    dq_t = nn(keys.T, dscores[...]) * FACTOR
    for h in range(GROUP):
        cols = pl.ds(h * HEAD_SIZE, HEAD_SIZE)
        dq_ref[at(i, BLOCK_TOKENS), cols] = (
            dq_t[:, h * HEAD_SIZE : (h + 1) * HEAD_SIZE].T.astype(jnp.bfloat16)
        )


def order_requests(sel_row, order):
    lane = lax.broadcasted_iota(jnp.int32, (1, SLOTS), 1)
    key = jnp.where(lax.rem(lane, CHOSEN_BLOCKS) == 0, BLOCKS * SLOTS, sel_row * SLOTS + lane)

    def column(x):
        return jnp.broadcast_to(x, (128, SLOTS)).T[:, :1]

    index = lax.broadcasted_iota(jnp.int32, (SLOTS, 1), 0)
    valid = lax.rem(index, CHOSEN_BLOCKS) != 0
    chosen = column(sel_row)
    rank = jnp.sum((key < column(key)).astype(jnp.int32), axis=1, keepdims=True)
    rank = jnp.where(valid, rank, -2)
    place = lax.div(index, CHOSEN_BLOCKS) * OTHERS + lax.rem(index, CHOSEN_BLOCKS) - 1

    def pick(mask, value):
        return jnp.sum(jnp.where(mask, value, 0), axis=0, keepdims=True)

    here = pick(rank == lane, chosen + 1)
    before = pick(rank + 1 == lane, chosen + 1)
    upto = pick(valid & (chosen <= lane), 1)
    count = pick(valid & (chosen == lane), 1)
    order[...] = jnp.zeros_like(order)
    order[0:1, :] = pick(rank == lane, place)
    order[1:2, :] = (here == before).astype(jnp.int32)
    order[2:3, :] = jnp.where(count > 0, upto - 1, REQUESTS)


def whole_kernel(
    sel, sel_row, k, v, q, g, dq, dk, dv,
    kz, vz, qh, gh, tab_k, tab_v, out_k, out_v, in_k, in_v, dk_out, dv_out, ret_k, ret_v, probs, dscores,
    dk_own, dv_own, runs, rs_out, rs_in, fin_out, fin_in, order_v, order,
    z_send, z_recv, s_send, s_recv, ag_send, ag_recv, k_send, k_recv, v_send, v_recv,
    rv_send, rv_recv, rk_send, rk_recv, rs_send, rs_recv, u_send, u_recv, own_sem,
):
    y, c, z = lax.axis_index("y"), lax.axis_index("xc"), lax.axis_index("grp")

    def device(dy=0, dc=0, dz=0):
        return (lax.rem(y + dy + Y, Y), lax.rem(c + dc, C), lax.rem(z + dz, Z))

    def remote(src, dst, send, recv, target):
        return pltpu.make_async_remote_copy(
            src_ref=src, dst_ref=dst, send_sem=send, recv_sem=recv,
            device_id=target, device_id_type=pl.DeviceIdType.MESH,
        )

    barrier = pltpu.get_barrier_semaphore()
    partners = [device(dz=d) for d in range(1, Z)] + [device(dc=d) for d in range(1, C)]
    partners += [device(dy=1), device(dy=-1)]
    for p in partners:
        pl.semaphore_signal(barrier, inc=1, device_id=p, device_id_type=pl.DeviceIdType.MESH)
    pl.semaphore_wait(barrier, len(partners))

    by_head = ((k, HEAD_SIZE, kz), (v, HEAD_SIZE, vz), (q, WIDE, qh), (g, WIDE, gh))

    def z_copy(n, d):
        src, width, dst = by_head[n]
        to = lax.rem(z + d, Z)
        return remote(src.at[:, at(to, width)], dst.at[z], z_send.at[n, d], z_recv.at[n, d], device(dz=d))

    for n in range(2):
        for d in range(1, Z):
            z_copy(n, d).start()
    for src, width, dst in by_head:
        dst[z] = src[:, at(z, width)]

    mine = at(y * C + c, Z)
    to_table = ((kz, tab_k), (vz, tab_v))

    def s_copy(n, d):
        src, tab = to_table[n]
        to = lax.rem(c + d, C)
        return remote(src.at[:, at(to, ROWS)], tab.at[mine], s_send.at[n, d], s_recv.at[n, d], device(dc=d))

    for n in range(2):
        for d in range(1, Z):
            z_copy(n, d).wait_recv()
        for d in range(1, C):
            s_copy(n, d).start()
        src, tab = to_table[n]
        tab[mine] = src[:, at(c, ROWS)]
    for n in (2, 3):
        for d in range(1, Z):
            z_copy(n, d).start()

    def ring(n, s, way, half):
        tab = to_table[n][1]
        owner = lax.rem(y - way * s + Y, Y)
        part = tab.at[at(owner * 2 + half, HALF)]
        lane = 0 if way > 0 else 1
        return remote(part, part, ag_send.at[n, s, lane, half], ag_recv.at[n, s, lane, half], device(dy=way))

    ring_order = ((1, 0), (-1, 1), (1, 1), (-1, 0))

    def ring_first(n):
        for way, half in ring_order:
            ring(n, 0, way, half).start()

    def ring_next(n, s):
        for way, half in ring_order[: 2 if s == STEPS - 1 else 4]:
            ring(n, s - 1, way, half).wait_recv()
            ring(n, s, way, half).start()

    def ring_last(n):
        for way, half in ring_order[2:]:
            ring(n, STEPS - 2, way, half).wait_recv()
        for way, half in ring_order[:2]:
            ring(n, STEPS - 1, way, half).wait_recv()

    def pack(tab, out, own, first, count):
        for d in range(C):
            to = lax.rem(c + d, C)

            @pl.loop(first, first + count)
            def _(i):
                for j in range(OTHERS):
                    rows = tab[sel[(to * Z + i) * CHOSEN_BLOCKS + 1 + j]]
                    if d:
                        out[d, i * OTHERS + j] = rows
                    else:
                        own[c, i * OTHERS + j] = rows

    def k_copy(d):
        return remote(out_k.at[d], in_k.at[c], k_send.at[d], k_recv.at[d], device(dc=d))

    part = UNITS // SPLITS

    def v_copy(d, n):
        span = pl.ds(n * part, part)
        return remote(out_v.at[d, span], in_v.at[c, span], v_send.at[d, n], v_recv.at[d, n], device(dc=d))

    def rv_copy(d, n):
        to = lax.rem(c + d, C)
        return remote(
            dv_out.at[to, pl.ds(n * part, part)], ret_v.at[pl.ds(c * UNITS + n * part, part)],
            rv_send.at[d, n], rv_recv.at[d, n], device(dc=d),
        )

    def rk_copy(d):
        to = lax.rem(c + d, C)
        return remote(dk_out.at[to], ret_k.at[at(c, UNITS)], rk_send.at[d], rk_recv.at[d], device(dc=d))

    for d in range(1, C):
        s_copy(0, d).wait_recv()
    ring_first(0)
    for d in range(1, C):
        s_copy(1, d).wait_recv()
    for s in range(1, STEPS):
        ring_next(0, s)
    ring_first(1)
    ring_last(0)
    pack(tab_k, out_k, in_k, 0, Z)
    for d in range(1, C):
        k_copy(d).start()
    for s in range(1, STEPS):
        ring_next(1, s)
    order_requests(sel_row[...], order_v)
    to_scalars = pltpu.make_async_copy(order_v, order, own_sem.at[2])
    to_scalars.start()
    to_scalars.wait()
    ring_last(1)

    for n in range(SPLITS):
        pack(tab_v, out_v, in_v, n * PER_SPLIT, PER_SPLIT)
        for d in range(1, C):
            v_copy(d, n).start()

    for n in (2, 3):
        for d in range(1, Z):
            z_copy(n, d).wait_recv()
    for d in range(1, C):
        k_copy(d).wait_recv()

    @pl.loop(0, SPLITS)
    def _(n):
        for d in range(1, C):
            v_copy(d, n).wait_recv()

        @pl.loop(0, PER_SPLIT)
        def _(m):
            i = n * PER_SPLIT + m
            first = (c * Z + i) * CHOSEN_BLOCKS
            attention_block(
                i, sel[first], lambda j: sel[first + j],
                qh, gh, kz, vz, in_k, in_v, dq, dk_own, dv_own, dk_out, dv_out, probs, dscores,
            )

        for d in range(1, C):
            rv_copy(d, n).start()

    for d in range(1, C):
        rk_copy(d).start()
    own_v = pltpu.make_async_copy(dv_out.at[c], ret_v.at[at(c, UNITS)], own_sem.at[0])
    own_k = pltpu.make_async_copy(dk_out.at[c], ret_k.at[at(c, UNITS)], own_sem.at[1])
    own_v.start()
    own_k.start()
    own_v.wait()
    own_k.wait()

    nothing = jnp.zeros((ROWS, HEAD_SIZE), jnp.float32)
    runs[REQUESTS] = nothing

    def run_sums(ret):
        def add(p, total):
            total = ret[order[0, p]].astype(jnp.float32) + jnp.where(order[1, p] == 1, total, 0.0)
            runs[p] = total
            return total

        lax.fori_loop(0, REQUESTS, add, nothing, unroll=8)

    def rs_copy(n, s, way, half):
        lane = 0 if way > 0 else 1
        return remote(
            rs_out.at[n, lane, s, half], rs_in.at[n, lane, s, half],
            rs_send.at[n, lane, s, half], rs_recv.at[n, lane, s, half], device(dy=way),
        )

    def rs_step(n, s, way, half, arrived):
        lane = 0 if way > 0 else 1
        owner = lax.rem(y + way * (STEPS - s) + Y, Y)
        if arrived:
            rs_copy(n, s - 1, way, half).wait_recv()

        @pl.loop(0, HALF, unroll=8)
        def _(t):
            total = runs[order[2, owner * SHARE + half * HALF + t]]
            if arrived:
                total += rs_in[n, lane, s - 1, half, t].astype(jnp.float32)
            rs_out[n, lane, s, half, t] = total.astype(jnp.bfloat16)

        rs_copy(n, s, way, half).start()

    def u_copy(n, d):
        to = lax.rem(c + d, C)
        return remote(
            fin_out.at[n, at(to, Z)], fin_in.at[n, :, at(c, ROWS)], u_send.at[n, d], u_recv.at[n, d], device(dc=d)
        )

    def reduce(n):
        for way, half in ring_order[:2]:
            rs_step(n, 0, way, half, False)
        for way, half in ring_order[2:]:
            rs_step(n, 1, way, half, False)
        for way, half in ring_order[:2]:
            rs_step(n, 1, way, half, True)
        for s in range(2, STEPS):
            for way, half in ring_order[2:] + ring_order[:2]:
                rs_step(n, s, way, half, True)
        for half in (1, 0):
            for way in (1, -1):
                rs_copy(n, STEPS - 1, way, half).wait_recv()

            @pl.loop(0, HALF, unroll=8)
            def _(t):
                total = runs[order[2, y * SHARE + half * HALF + t]]
                for lane in range(2):
                    total += rs_in[n, lane, STEPS - 1, half, t].astype(jnp.float32)
                fin_out[n, half * HALF + t] = total.astype(jnp.bfloat16)

        for d in range(1, C):
            u_copy(n, d).start()
        fin_in[n, :, at(c, ROWS)] = fin_out[n, at(c, Z)]

    for n in range(SPLITS):
        for d in range(1, C):
            rv_copy(d, n).wait_recv()
    run_sums(ret_v)
    reduce(1)
    for d in range(1, C):
        rk_copy(d).wait_recv()
    run_sums(ret_k)
    reduce(0)
    for n, own, out in ((1, dv_own, dv), (0, dk_own, dk)):
        for d in range(1, C):
            u_copy(n, d).wait_recv()
        for i in range(Z):
            out[i] = (fin_in[n, i].astype(jnp.float32) + own[i]).astype(jnp.bfloat16)

    for d in range(1, Z):
        for n in range(4):
            z_copy(n, d).wait_send()
    for d in range(1, C):
        for n in range(2):
            s_copy(n, d).wait_send()
            u_copy(n, d).wait_send()
        k_copy(d).wait_send()
        rk_copy(d).wait_send()
        for n in range(SPLITS):
            v_copy(d, n).wait_send()
            rv_copy(d, n).wait_send()
    for n in range(2):
        for s in range(STEPS):
            for way, half in ring_order[: 2 if s == STEPS - 1 else 4]:
                ring(n, s, way, half).wait_send()
            for way, half in ring_order[: 2 if s == 0 else 4]:
                rs_copy(n, s, way, half).wait_send()


def whole(sel, k, v, q, g):
    vmem = pl.BlockSpec(memory_space=pltpu.VMEM)
    bf16 = lambda *shape: pltpu.VMEM(shape, jnp.bfloat16)
    f32 = lambda *shape: pltpu.VMEM(shape, jnp.float32)
    dma = lambda *shape: pltpu.SemaphoreType.DMA(shape)
    units = (C, UNITS, ROWS, HEAD_SIZE)
    table = (BLOCKS, ROWS, HEAD_SIZE)
    heads = (Z, BLOCK_TOKENS, HEAD_SIZE)
    steps = (2, 2, STEPS, 2, HALF, ROWS, HEAD_SIZE)
    return pl.pallas_call(
        whole_kernel,
        out_shape=(
            jax.ShapeDtypeStruct((Z * BLOCK_TOKENS, WIDE), jnp.bfloat16),
            jax.ShapeDtypeStruct(heads, jnp.bfloat16),
            jax.ShapeDtypeStruct(heads, jnp.bfloat16),
        ),
        in_specs=[pl.BlockSpec(memory_space=pltpu.SMEM)] + [vmem] * 5,
        out_specs=[vmem] * 3,
        scratch_shapes=[bf16(*heads)] * 2
        + [bf16(Z, BLOCK_TOKENS, WIDE)] * 2
        + [bf16(*table)] * 2
        + [bf16(*units)] * 6
        + [bf16(REQUESTS, ROWS, HEAD_SIZE)] * 2
        + [bf16(KEYS, WIDE)] * 2
        + [f32(*heads)] * 2
        + [f32(REQUESTS + 8, ROWS, HEAD_SIZE)]
        + [bf16(*steps)] * 2
        + [bf16(2, SHARE, ROWS, HEAD_SIZE)]
        + [bf16(2, *heads)]
        + [pltpu.VMEM((8, SLOTS), jnp.int32), pltpu.SMEM((8, SLOTS), jnp.int32)]
        + [dma(4, Z)] * 2
        + [dma(2, C)] * 2
        + [dma(2, STEPS, 2, 2)] * 2
        + [dma(C)] * 2
        + [dma(C, SPLITS)] * 2
        + [dma(C, SPLITS)] * 2
        + [dma(C)] * 2
        + [dma(2, 2, STEPS, 2)] * 2
        + [dma(2, C)] * 2
        + [dma(3)],
        compiler_params=pltpu.CompilerParams(
            vmem_limit_bytes=VMEM, collective_id=0, has_side_effects=True
        ),
        name="whole",
    )(sel, sel.reshape(1, SLOTS), k, v, q, g)


def body(query, keys, values, output_cotangent, select):
    row = lax.axis_index("y")
    flat = select.reshape(BLOCKS * CHOSEN_BLOCKS)
    row_select = lax.dynamic_slice_in_dim(flat, row * SLOTS, SLOTS, 0)
    dq, dk, dv = whole(row_select, keys, values, query, output_cotangent)
    rows = (Z * BLOCK_TOKENS, HEAD_SIZE)
    return dq, dk.reshape(rows), dv.reshape(rows)


def solution(mesh):
    groups = mesh.shape["grp"]
    grid = jax.sharding.Mesh(
        mesh.devices.reshape(-1, STRIPES, groups), ("y", "xc", "grp")
    )
    rows = ("y", "xc")
    in_specs = (P(rows + ("grp",), None),) * 4 + (P(None, "grp", None),)
    out_specs = (P(rows, "grp"),) * 3
    return jax.shard_map(
        body, mesh=grid, in_specs=in_specs, out_specs=out_specs, check_vma=False
    )
```

```python
import functools

import jax
import jax.numpy as jnp
from jax import lax
from jax.experimental import pallas as pl
from jax.experimental.pallas import tpu as pltpu
from jax.sharding import PartitionSpec as P

HEAD_SIZE = 128
QUERY_HEADS = 32
KEY_HEADS = 8
BLOCK_TOKENS = 128
CHOSEN_BLOCKS = 8
GROUP = QUERY_HEADS // KEY_HEADS
STRIPES = 8
ROWS = BLOCK_TOKENS // STRIPES
KEYS = CHOSEN_BLOCKS * BLOCK_TOKENS
FACTOR = HEAD_SIZE ** (-0.5)
VMEM = 56 * 1024 * 1024


def nt(a, b):
    return lax.dot_general(a, b, (((1,), (1,)), ((), ())), preferred_element_type=jnp.float32)


def nn(a, b):
    return jnp.dot(a, b, preferred_element_type=jnp.float32)


Y, C, Z = 8, 8, 8
OTHERS = CHOSEN_BLOCKS - 1
OTHER_KEYS = OTHERS * BLOCK_TOKENS
UNITS = Z * OTHERS
REQUESTS = C * UNITS
SLOTS = C * Z * CHOSEN_BLOCKS
SHARE = C * Z
BLOCKS = Y * SHARE
PARTS = 4
PIECE = SHARE // PARTS
STEPS = 4
SPLITS = 4
PER_SPLIT = Z // SPLITS
WIDE = GROUP * HEAD_SIZE


def at(index, size):
    return pl.ds(pl.multiple_of(index * size, size), size)


def attention_block(
    i, own, sel_at, q_ref, g_ref, kz, vz, k_ref, v_ref, dq_ref, dk_own, dv_own, dk_ref, dv_ref, probs, dscores
):
    units = pl.ds(i * OTHERS, OTHERS)
    keys = jnp.concatenate([kz[i], k_ref[:, units].reshape(OTHER_KEYS, HEAD_SIZE)], 0)
    vals = jnp.concatenate([vz[i], v_ref[:, units].reshape(OTHER_KEYS, HEAD_SIZE)], 0)
    row = lax.broadcasted_iota(jnp.int32, (BLOCK_TOKENS, BLOCK_TOKENS), 0)
    token = lax.broadcasted_iota(jnp.int32, (BLOCK_TOKENS, BLOCK_TOKENS), 1)
    own_bias = jnp.where(row <= token, 0.0, -jnp.inf).astype(jnp.float32)
    other_bias = jnp.stack(
        [
            jnp.full(
                (STRIPES, ROWS, BLOCK_TOKENS), jnp.where(sel_at(j) < own, 0.0, -jnp.inf), jnp.float32
            )
            for j in range(1, CHOSEN_BLOCKS)
        ],
        axis=1,
    ).reshape(OTHER_KEYS, BLOCK_TOKENS)
    bias = jnp.concatenate([own_bias, other_bias], 0)
    q_parts, g_parts = [], []
    for h in range(GROUP):
        cols = pl.ds(h * HEAD_SIZE, HEAD_SIZE)
        q, g = q_ref[i, :, cols], g_ref[i, :, cols]
        q_parts.append(q)
        g_parts.append(g)
        scores = nt(keys, q) * FACTOR + bias
        highest = jnp.max(scores, axis=0, keepdims=True)
        weights = jnp.exp(scores - highest)
        prob = weights * (1.0 / jnp.sum(weights, axis=0, keepdims=True))
        low = prob.astype(jnp.bfloat16)
        dprobs = nt(vals, g)
        delta = jnp.sum(low.astype(jnp.float32) * dprobs, axis=0, keepdims=True)
        probs[:, cols] = low
        dscores[:, cols] = (prob * (dprobs - delta)).astype(jnp.bfloat16)
    others = (STRIPES, OTHERS, ROWS, HEAD_SIZE)
    dv = nn(probs[...], jnp.concatenate(g_parts, 0))
    dv_own[i] = dv[:BLOCK_TOKENS]
    dv_ref[:, units] = dv[BLOCK_TOKENS:].astype(jnp.bfloat16).reshape(others)
    dk = nn(dscores[...], jnp.concatenate(q_parts, 0)) * FACTOR
    dk_own[i] = dk[:BLOCK_TOKENS]
    dk_ref[:, units] = dk[BLOCK_TOKENS:].astype(jnp.bfloat16).reshape(others)
    dq_t = nn(keys.T, dscores[...]) * FACTOR
    for h in range(GROUP):
        cols = pl.ds(h * HEAD_SIZE, HEAD_SIZE)
        dq_ref[at(i, BLOCK_TOKENS), cols] = (
            dq_t[:, h * HEAD_SIZE : (h + 1) * HEAD_SIZE].T.astype(jnp.bfloat16)
        )


def order_requests(sel_row, order):
    lane = lax.broadcasted_iota(jnp.int32, (1, SLOTS), 1)
    key = jnp.where(lane < SHARE, BLOCKS * SLOTS, sel_row * SLOTS + lane)

    def column(x):
        return jnp.broadcast_to(x, (128, SLOTS)).T[:, :1]

    index = lax.broadcasted_iota(jnp.int32, (SLOTS, 1), 0)
    valid = index >= SHARE
    chosen = column(sel_row)
    rank = jnp.sum((key < column(key)).astype(jnp.int32), axis=1, keepdims=True)
    rank = jnp.where(valid, rank, -2)
    place = lax.rem(index, SHARE) * OTHERS + lax.div(index, SHARE) - 1

    def pick(mask, value):
        return jnp.sum(jnp.where(mask, value, 0), axis=0, keepdims=True)

    here = pick(rank == lane, chosen + 1)
    before = pick(rank + 1 == lane, chosen + 1)
    upto = pick(valid & (chosen <= lane), 1)
    count = pick(valid & (chosen == lane), 1)
    order[...] = jnp.zeros_like(order)
    order[0:1, :] = pick(rank == lane, place)
    order[1:2, :] = (here == before).astype(jnp.int32)
    order[2:3, :] = jnp.where(count > 0, upto - 1, REQUESTS)


def whole_kernel(
    sel, sel_rows, k, v, q, g, dq, dk, dv,
    kz, vz, qh, gh, tab_k, tab_v, out_k, out_v, in_k, in_v, dk_out, dv_out, ret_k, ret_v, probs, dscores,
    dk_own, dv_own, k_runs, v_runs, rs_out, rs_in, fin_out, fin_in, order_v, order,
    z_send, z_recv, s_send, s_recv, ag_send, ag_recv, k_send, k_recv, v_send, v_recv,
    rv_send, rv_recv, rk_send, rk_recv, rs_send, rs_recv, u_send, u_recv, own_sem, d_sem, l_send, l_recv,
):
    y, c, z = lax.axis_index("y"), lax.axis_index("xc"), lax.axis_index("grp")

    def device(dy=0, dc=0, dz=0):
        return (lax.rem(y + dy + Y, Y), lax.rem(c + dc, C), lax.rem(z + dz, Z))

    def remote(src, dst, send, recv, target):
        return pltpu.make_async_remote_copy(
            src_ref=src, dst_ref=dst, send_sem=send, recv_sem=recv,
            device_id=target, device_id_type=pl.DeviceIdType.MESH,
        )

    barrier = pltpu.get_barrier_semaphore()
    partners = [device(dc=e, dz=d) for e in range(C) for d in range(Z) if e or d]
    partners += [device(dy=way, dc=e) for way in (1, -1) for e in range(C)]
    for p in partners:
        pl.semaphore_signal(barrier, inc=1, device_id=p, device_id_type=pl.DeviceIdType.MESH)
    pl.semaphore_wait(barrier, len(partners))

    by_head = (None, (v, HEAD_SIZE, vz), (q, WIDE, qh), (g, WIDE, gh))

    def z_copy(n, d):
        src, width, dst = by_head[n]
        to = lax.rem(z + d, Z)
        return remote(src.at[:, at(to, width)], dst.at[z], z_send.at[n, d], z_recv.at[n, d], device(dz=d))

    def keys_copy(e, d):
        to, head = lax.rem(c + e, C), lax.rem(z + d, Z)
        return remote(
            k.at[at(to, ROWS), at(head, HEAD_SIZE)], tab_k.at[y * SHARE + c * Z + z],
            d_sem.at[0], d_sem.at[1], device(dc=e, dz=d),
        )

    def keys_all():
        all_but_one = tab_k.at[pl.ds(0, SHARE - 1)]
        return remote(all_but_one, all_but_one, d_sem.at[0], d_sem.at[1], device(dc=1))

    for d in range(Z):
        for e in range(C):
            if d or e:
                keys_copy(e, d).start()
    for n in range(1, 4):
        for d in range(1, Z):
            z_copy(n, d).start()
    tab_k[y * SHARE + c * Z + z] = k[at(c, ROWS), at(z, HEAD_SIZE)]
    vz[z] = v[:, at(z, HEAD_SIZE)]
    own_q = pltpu.make_async_copy(q.at[:, at(z, WIDE)], qh.at[z], own_sem.at[3])
    own_g = pltpu.make_async_copy(g.at[:, at(z, WIDE)], gh.at[z], own_sem.at[4])
    own_q.start()
    own_g.start()

    mine = at(y * C + c, Z)

    def s_copy(n, d):
        to = lax.rem(c + d, C)
        if n:
            src, dst = vz.at[:, at(to, ROWS)], tab_v.at[mine]
        else:
            src, dst = tab_k.at[at(y * C + to, Z)], kz.at[:, at(c, ROWS)]
        return remote(src, dst, s_send.at[n, d], s_recv.at[n, d], device(dc=d))

    def ring(n, s, way, half):
        tab = (tab_k, tab_v)[n]
        owner = lax.rem(y - way * s + Y, Y)
        part = tab.at[at(owner * PARTS + half, PIECE)]
        lane = 0 if way > 0 else 1
        return remote(part, part, ag_send.at[n, s, lane, half], ag_recv.at[n, s, lane, half], device(dy=way))

    ring_order = []
    for n in range(PARTS):
        ring_order += [(1, n), (-1, (n + PARTS // 2) % PARTS)]

    def ring_first(n):
        for way, half in ring_order:
            ring(n, 0, way, half).start()

    def ring_next(n, s):
        for way, half in ring_order[: PARTS if s == STEPS - 1 else 2 * PARTS]:
            ring(n, s - 1, way, half).wait_recv()
            ring(n, s, way, half).start()

    def ring_last(n):
        for way, half in ring_order[PARTS:]:
            ring(n, STEPS - 2, way, half).wait_recv()
        for way, half in ring_order[:PARTS]:
            ring(n, STEPS - 1, way, half).wait_recv()

    def chosen_row():
        two = sel_rows[:, at(lax.div(y, 2), 2 * SHARE)]
        turned = pltpu.roll(two, SHARE, 1)
        low = jnp.where(lax.rem(y, 2) == 0, two, turned)
        high = jnp.where(lax.rem(y, 2) == 0, turned, two)
        lane = lax.broadcasted_iota(jnp.int32, (1, 2 * SHARE), 1)
        return jnp.concatenate(
            [
                jnp.where(lane < SHARE, low[j : j + 1], high[j + 1 : j + 2])
                for j in range(0, CHOSEN_BLOCKS, 2)
            ],
            axis=1,
        )

    def pack(tab, out, own, first, count):
        for d in range(C):
            to = lax.rem(c + d, C)

            @pl.loop(first, first + count)
            def _(i):
                for j in range(OTHERS):
                    rows = tab[sel[1 + j, y * SHARE + to * Z + i]]
                    if d:
                        out[d, i * OTHERS + j] = rows
                    else:
                        own[c, i * OTHERS + j] = rows

    def k_copy(d):
        return remote(out_k.at[d], in_k.at[c], k_send.at[d], k_recv.at[d], device(dc=d))

    part = UNITS // SPLITS

    def v_copy(d, n):
        span = pl.ds(n * part, part)
        return remote(out_v.at[d, span], in_v.at[c, span], v_send.at[d, n], v_recv.at[d, n], device(dc=d))

    def rv_copy(d, n):
        to = lax.rem(c + d, C)
        return remote(
            dv_out.at[to, pl.ds(n * part, part)], ret_v.at[pl.ds(c * UNITS + n * part, part)],
            rv_send.at[d, n], rv_recv.at[d, n], device(dc=d),
        )

    def rk_copy(d):
        to = lax.rem(c + d, C)
        return remote(dk_out.at[to], ret_k.at[at(c, UNITS)], rk_send.at[d], rk_recv.at[d], device(dc=d))

    keys_all().wait_recv()
    ring_first(0)
    for d in range(1, C):
        s_copy(0, d).start()
    kz[:, at(c, ROWS)] = tab_k[mine]
    for d in range(1, Z):
        z_copy(1, d).wait_recv()
    for d in range(1, C):
        s_copy(1, d).start()
    tab_v[mine] = vz[:, at(c, ROWS)]
    for s in range(1, STEPS):
        ring_next(0, s)
    for d in range(1, C):
        s_copy(1, d).wait_recv()
    ring_first(1)
    ring_last(0)
    pack(tab_k, out_k, in_k, 0, Z)
    for d in range(1, C):
        k_copy(d).start()
    for s in range(1, STEPS):
        ring_next(1, s)
    order_requests(chosen_row(), order_v)
    to_scalars = pltpu.make_async_copy(order_v, order, own_sem.at[2])
    to_scalars.start()
    to_scalars.wait()
    ring_last(1)

    for n in range(SPLITS):
        pack(tab_v, out_v, in_v, n * PER_SPLIT, PER_SPLIT)
        for d in range(1, C):
            v_copy(d, n).start()

    own_q.wait()
    own_g.wait()
    for n in (2, 3):
        for d in range(1, Z):
            z_copy(n, d).wait_recv()
    for d in range(1, C):
        s_copy(0, d).wait_recv()
        k_copy(d).wait_recv()

    @pl.loop(0, SPLITS)
    def _(n):
        for d in range(1, C):
            v_copy(d, n).wait_recv()

        @pl.loop(0, PER_SPLIT)
        def _(m):
            i = n * PER_SPLIT + m
            block = y * SHARE + c * Z + i
            attention_block(
                i, block, lambda j: sel[j, block],
                qh, gh, kz, vz, in_k, in_v, dq, dk_own, dv_own, dk_out, dv_out, probs, dscores,
            )

        for d in range(1, C):
            rv_copy(d, n).start()

    for d in range(1, C):
        rk_copy(d).start()
    own_v = pltpu.make_async_copy(dv_out.at[c], ret_v.at[at(c, UNITS)], own_sem.at[0])
    own_k = pltpu.make_async_copy(dk_out.at[c], ret_k.at[at(c, UNITS)], own_sem.at[1])
    own_v.start()
    own_k.start()
    own_v.wait()
    own_k.wait()

    nothing = jnp.zeros((ROWS, HEAD_SIZE), jnp.float32)
    all_runs = (k_runs, v_runs)

    def run_sums(ret, runs):
        runs[REQUESTS] = nothing

        def add(p, total):
            total = ret[order[0, p]].astype(jnp.float32) + jnp.where(order[1, p] == 1, total, 0.0)
            runs[p] = total
            return total

        lax.fori_loop(0, REQUESTS, add, nothing, unroll=8)

    def rs_copy(n, s, way, half):
        lane = 0 if way > 0 else 1
        return remote(
            rs_out.at[n, lane, s, half], rs_in.at[n, lane, s, half],
            rs_send.at[n, lane, s, half], rs_recv.at[n, lane, s, half], device(dy=way),
        )

    def rs_step(n, s, way, half, arrived):
        lane = 0 if way > 0 else 1
        owner = lax.rem(y + way * (STEPS - s) + Y, Y)
        if arrived:
            rs_copy(n, s - 1, way, half).wait_recv()

        @pl.loop(0, PIECE, unroll=8)
        def _(t):
            total = all_runs[n][order[2, owner * SHARE + half * PIECE + t]]
            if arrived:
                total += rs_in[n, lane, s - 1, half, t].astype(jnp.float32)
            rs_out[n, lane, s, half, t] = total.astype(jnp.bfloat16)

        if s < STEPS - 1:
            rs_copy(n, s, way, half).start()
        else:
            for m in range(C // PARTS):
                last_copy(n, way, half, m).start()

    def last_copy(n, way, half, m):
        lane = 0 if way > 0 else 1
        to = half * (C // PARTS) + m
        e = lax.rem(to - c + C, C)
        return remote(
            rs_out.at[n, lane, STEPS - 1, half, pl.ds(m * Z, Z)], fin_in.at[n, lane, :, at(c, ROWS)],
            l_send.at[n, lane, e], l_recv.at[n, lane, e], (lax.rem(y + way + Y, Y), to, z),
        )

    def u_copy(n, d):
        to = lax.rem(c + d, C)
        return remote(
            fin_out.at[n, at(to, Z)], fin_in.at[n, 2, :, at(c, ROWS)], u_send.at[n, d], u_recv.at[n, d], device(dc=d)
        )

    def reduce_own(n):
        @pl.loop(0, SHARE, unroll=8)
        def _(t):
            fin_out[n, t] = all_runs[n][order[2, y * SHARE + t]].astype(jnp.bfloat16)

        for d in range(1, C):
            u_copy(n, d).start()
        fin_in[n, 2, :, at(c, ROWS)] = fin_out[n, at(c, Z)]

    def reduce_first(n):
        for way, half in ring_order[:PARTS]:
            rs_step(n, 0, way, half, False)
        for way, half in ring_order[PARTS:]:
            rs_step(n, 1, way, half, False)

    def reduce_next(n):
        for way, half in ring_order[:PARTS]:
            rs_step(n, 1, way, half, True)
        for s in range(2, STEPS):
            for way, half in ring_order[PARTS:] + ring_order[:PARTS]:
                rs_step(n, s, way, half, True)

    for n in range(SPLITS):
        for d in range(1, C):
            rv_copy(d, n).wait_recv()
    run_sums(ret_v, v_runs)
    reduce_first(1)
    reduce_own(1)
    reduce_next(1)
    for d in range(1, C):
        rk_copy(d).wait_recv()
    run_sums(ret_k, k_runs)
    reduce_first(0)
    reduce_own(0)
    reduce_next(0)
    for n, own, out in ((1, dv_own, dv), (0, dk_own, dk)):
        for d in range(1, C):
            u_copy(n, d).wait_recv()
        for way in (1, -1):
            for half in range(PARTS):
                for m in range(C // PARTS):
                    last_copy(n, way, half, m).wait_recv()
        for i in range(Z):
            total = own[i]
            for lane in range(3):
                total += fin_in[n, lane, i].astype(jnp.float32)
            out[i] = total.astype(jnp.bfloat16)

    keys_all().wait_send()
    for d in range(1, Z):
        for n in range(1, 4):
            z_copy(n, d).wait_send()
    for d in range(1, C):
        for n in range(2):
            s_copy(n, d).wait_send()
            u_copy(n, d).wait_send()
        k_copy(d).wait_send()
        rk_copy(d).wait_send()
        for n in range(SPLITS):
            v_copy(d, n).wait_send()
            rv_copy(d, n).wait_send()
    for n in range(2):
        for s in range(STEPS):
            for way, half in ring_order[: PARTS if s == STEPS - 1 else 2 * PARTS]:
                ring(n, s, way, half).wait_send()
            for way, half in ring_order[: PARTS if s == 0 else 2 * PARTS]:
                if s < STEPS - 1:
                    rs_copy(n, s, way, half).wait_send()
                else:
                    for m in range(C // PARTS):
                        last_copy(n, way, half, m).wait_send()


def whole(sel, k, v, q, g):
    vmem = pl.BlockSpec(memory_space=pltpu.VMEM)
    bf16 = lambda *shape: pltpu.VMEM(shape, jnp.bfloat16)
    f32 = lambda *shape: pltpu.VMEM(shape, jnp.float32)
    dma = lambda *shape: pltpu.SemaphoreType.DMA(shape)
    units = (C, UNITS, ROWS, HEAD_SIZE)
    table = (BLOCKS, ROWS, HEAD_SIZE)
    heads = (Z, BLOCK_TOKENS, HEAD_SIZE)
    steps = (2, 2, STEPS, PARTS, PIECE, ROWS, HEAD_SIZE)
    return pl.pallas_call(
        whole_kernel,
        out_shape=(
            jax.ShapeDtypeStruct((Z * BLOCK_TOKENS, WIDE), jnp.bfloat16),
            jax.ShapeDtypeStruct(heads, jnp.bfloat16),
            jax.ShapeDtypeStruct(heads, jnp.bfloat16),
        ),
        in_specs=[pl.BlockSpec(memory_space=pltpu.SMEM)] + [vmem] * 3 + [pl.BlockSpec(memory_space=pl.ANY)] * 2,
        out_specs=[vmem] * 3,
        scratch_shapes=[bf16(*heads)] * 2
        + [bf16(Z, BLOCK_TOKENS, WIDE)] * 2
        + [bf16(*table)] * 2
        + [bf16(*units)] * 6
        + [bf16(REQUESTS, ROWS, HEAD_SIZE)] * 2
        + [bf16(KEYS, WIDE)] * 2
        + [f32(*heads)] * 2
        + [f32(REQUESTS + 8, ROWS, HEAD_SIZE)] * 2
        + [bf16(*steps)] * 2
        + [bf16(2, SHARE, ROWS, HEAD_SIZE)]
        + [bf16(2, 3, *heads)]
        + [pltpu.VMEM((8, SLOTS), jnp.int32), pltpu.SMEM((8, SLOTS), jnp.int32)]
        + [dma(4, Z)] * 2
        + [dma(2, C)] * 2
        + [dma(2, STEPS, 2, PARTS)] * 2
        + [dma(C)] * 2
        + [dma(C, SPLITS)] * 2
        + [dma(C, SPLITS)] * 2
        + [dma(C)] * 2
        + [dma(2, 2, STEPS, PARTS)] * 2
        + [dma(2, C)] * 2
        + [dma(5)]
        + [dma(2)]
        + [dma(2, 2, C)] * 2,
        compiler_params=pltpu.CompilerParams(
            vmem_limit_bytes=VMEM, collective_id=0, has_side_effects=True
        ),
        name="whole",
    )(sel, sel, k, v, q, g)


def finish_kernel(dq, dk, dv, dq_out, dk_out, dv_out):
    dq_out[...] = dq[...]
    dk_out[...] = dk[...]
    dv_out[...] = dv[...]


def finish(*arrays):
    vmem = pl.BlockSpec(memory_space=pltpu.VMEM)
    return pl.pallas_call(
        finish_kernel,
        out_shape=tuple(jax.ShapeDtypeStruct(a.shape, a.dtype) for a in arrays),
        in_specs=[vmem] * len(arrays),
        out_specs=[vmem] * len(arrays),
        compiler_params=pltpu.CompilerParams(vmem_limit_bytes=VMEM),
        name="finish",
    )(*arrays)


def body(query, keys, values, output_cotangent, select):
    by_slot = select.reshape(BLOCKS, CHOSEN_BLOCKS).T
    dq, dk, dv = finish(*whole(by_slot, keys, values, query, output_cotangent))
    rows = (Z * BLOCK_TOKENS, HEAD_SIZE)
    return dq, dk.reshape(rows), dv.reshape(rows)


def solution(mesh):
    groups = mesh.shape["grp"]
    grid = jax.sharding.Mesh(
        mesh.devices.reshape(-1, STRIPES, groups), ("y", "xc", "grp")
    )
    rows = ("y", "xc")
    in_specs = (P(rows + ("grp",), None),) * 4 + (P(None, "grp", None),)
    out_specs = (P(rows, "grp"),) * 3
    return jax.shard_map(
        body, mesh=grid, in_specs=in_specs, out_specs=out_specs, check_vma=False
    )
```

```python
import functools

import jax
import jax.numpy as jnp
from jax import lax
from jax.experimental import pallas as pl
from jax.experimental.pallas import tpu as pltpu
from jax.sharding import PartitionSpec as P

HEAD_SIZE = 128
QUERY_HEADS = 32
KEY_HEADS = 8
BLOCK_TOKENS = 128
CHOSEN_BLOCKS = 8
GROUP = QUERY_HEADS // KEY_HEADS
STRIPES = 8
ROWS = BLOCK_TOKENS // STRIPES
KEYS = CHOSEN_BLOCKS * BLOCK_TOKENS
FACTOR = HEAD_SIZE ** (-0.5)
VMEM = 56 * 1024 * 1024


def nt(a, b):
    return lax.dot_general(a, b, (((1,), (1,)), ((), ())), preferred_element_type=jnp.float32)


def nn(a, b):
    return jnp.dot(a, b, preferred_element_type=jnp.float32)


Y, C, Z = 8, 8, 8
OTHERS = CHOSEN_BLOCKS - 1
OTHER_KEYS = OTHERS * BLOCK_TOKENS
UNITS = Z * OTHERS
REQUESTS = C * UNITS
SLOTS = C * Z * CHOSEN_BLOCKS
SHARE = C * Z
BLOCKS = Y * SHARE
PARTS = 4
PIECE = SHARE // PARTS
STEPS = 4
TURN_STEP = 2
SPLITS = 4
PER_SPLIT = Z // SPLITS
WIDE = GROUP * HEAD_SIZE
OTHERS_SHAPE = (STRIPES, OTHERS, ROWS, HEAD_SIZE)


def at(index, size):
    return pl.ds(pl.multiple_of(index * size, size), size)


def probs_block(i, own, sel_at, q_ref, g_ref, kz, k_ref, dv_own, dv_ref, probs):
    units = pl.ds(i * OTHERS, OTHERS)
    keys = jnp.concatenate([kz[i], k_ref[:, units].reshape(OTHER_KEYS, HEAD_SIZE)], 0)
    row = lax.broadcasted_iota(jnp.int32, (BLOCK_TOKENS, BLOCK_TOKENS), 0)
    token = lax.broadcasted_iota(jnp.int32, (BLOCK_TOKENS, BLOCK_TOKENS), 1)
    own_bias = jnp.where(row <= token, 0.0, -jnp.inf).astype(jnp.float32)
    other_bias = jnp.stack(
        [
            jnp.full(
                (STRIPES, ROWS, BLOCK_TOKENS), jnp.where(sel_at(j) < own, 0.0, -jnp.inf), jnp.float32
            )
            for j in range(1, CHOSEN_BLOCKS)
        ],
        axis=1,
    ).reshape(OTHER_KEYS, BLOCK_TOKENS)
    bias = jnp.concatenate([own_bias, other_bias], 0)
    for h in range(GROUP):
        cols = pl.ds(h * HEAD_SIZE, HEAD_SIZE)
        scores = nt(keys, q_ref[i, :, cols]) * FACTOR + bias
        highest = jnp.max(scores, axis=0, keepdims=True)
        weights = jnp.exp(scores - highest)
        prob = weights * (1.0 / jnp.sum(weights, axis=0, keepdims=True))
        probs[i, :, cols] = prob.astype(jnp.bfloat16)
    dv = nn(probs[i], by_head_rows(g_ref, i))
    dv_own[i] = dv[:BLOCK_TOKENS]
    dv_ref[:, units] = dv[BLOCK_TOKENS:].astype(jnp.bfloat16).reshape(OTHERS_SHAPE)


def by_head_rows(ref, i):
    return jnp.concatenate([ref[i, :, h * HEAD_SIZE : (h + 1) * HEAD_SIZE] for h in range(GROUP)], 0)


def scores_block(i, q_ref, g_ref, kz, vz, k_ref, v_ref, dq_ref, dk_own, dk_ref, probs, dscores):
    units = pl.ds(i * OTHERS, OTHERS)
    keys = jnp.concatenate([kz[i], k_ref[:, units].reshape(OTHER_KEYS, HEAD_SIZE)], 0)
    vals = jnp.concatenate([vz[i], v_ref[:, units].reshape(OTHER_KEYS, HEAD_SIZE)], 0)
    for h in range(GROUP):
        cols = pl.ds(h * HEAD_SIZE, HEAD_SIZE)
        prob = probs[i, :, cols].astype(jnp.float32)
        dprobs = nt(vals, g_ref[i, :, cols])
        delta = jnp.sum(prob * dprobs, axis=0, keepdims=True)
        dscores[:, cols] = (prob * (dprobs - delta)).astype(jnp.bfloat16)
    dk = nn(dscores[...], by_head_rows(q_ref, i)) * FACTOR
    dk_own[i] = dk[:BLOCK_TOKENS]
    dk_ref[:, units] = dk[BLOCK_TOKENS:].astype(jnp.bfloat16).reshape(OTHERS_SHAPE)
    dq_t = nn(keys.T, dscores[...]) * FACTOR
    for h in range(GROUP):
        cols = pl.ds(h * HEAD_SIZE, HEAD_SIZE)
        dq_ref[at(i, BLOCK_TOKENS), cols] = (
            dq_t[:, h * HEAD_SIZE : (h + 1) * HEAD_SIZE].T.astype(jnp.bfloat16)
        )


def order_requests(sel_row, order):
    lane = lax.broadcasted_iota(jnp.int32, (1, SLOTS), 1)
    key = jnp.where(lane < SHARE, BLOCKS * SLOTS, sel_row * SLOTS + lane)

    def column(x):
        return jnp.broadcast_to(x, (128, SLOTS)).T[:, :1]

    index = lax.broadcasted_iota(jnp.int32, (SLOTS, 1), 0)
    valid = index >= SHARE
    chosen = column(sel_row)
    rank = jnp.sum((key < column(key)).astype(jnp.int32), axis=1, keepdims=True)
    rank = jnp.where(valid, rank, -2)
    place = lax.rem(index, SHARE) * OTHERS + lax.div(index, SHARE) - 1

    def pick(mask, value):
        return jnp.sum(jnp.where(mask, value, 0), axis=0, keepdims=True)

    here = pick(rank == lane, chosen + 1)
    before = pick(rank + 1 == lane, chosen + 1)
    upto = pick(valid & (chosen <= lane), 1)
    count = pick(valid & (chosen == lane), 1)
    order[...] = jnp.zeros_like(order)
    order[0:1, :] = pick(rank == lane, place)
    order[1:2, :] = (here == before).astype(jnp.int32)
    order[2:3, :] = jnp.where(count > 0, upto - 1, REQUESTS)


def whole_kernel(
    sel, sel_rows, k, v, q, g, dq, dk, dv,
    kz, vz, qh, gh, tab_k, tab_v, out_k, out_v, in_k, in_v, dk_out, dv_out, ret_k, ret_v, probs, dscores,
    dk_own, dv_own, runs, rs_out, rs_in, fin_out, fin_in, order_v, order,
    z_send, z_recv, s_send, s_recv, ag_send, ag_recv, k_send, k_recv, v_send, v_recv,
    rv_send, rv_recv, rk_send, rk_recv, rs_send, rs_recv, u_send, u_recv, own_sem, d_sem, l_send, l_recv, turn,
):
    y, c, z = lax.axis_index("y"), lax.axis_index("xc"), lax.axis_index("grp")

    def device(dy=0, dc=0, dz=0):
        return (lax.rem(y + dy + Y, Y), lax.rem(c + dc, C), lax.rem(z + dz, Z))

    def remote(src, dst, send, recv, target):
        return pltpu.make_async_remote_copy(
            src_ref=src, dst_ref=dst, send_sem=send, recv_sem=recv,
            device_id=target, device_id_type=pl.DeviceIdType.MESH,
        )

    tab_k[...] = jnp.zeros_like(tab_k)
    tab_v[...] = jnp.zeros_like(tab_v)

    barrier = pltpu.get_barrier_semaphore()
    partners = [device(dc=e, dz=d) for e in range(C) for d in range(Z) if e or d]
    partners += [device(dy=way, dc=e) for way in (1, -1) for e in range(C)]
    for p in partners:
        pl.semaphore_signal(barrier, inc=1, device_id=p, device_id_type=pl.DeviceIdType.MESH)
    pl.semaphore_wait(barrier, len(partners))

    by_head = (None, (v, HEAD_SIZE, vz), (q, WIDE, qh), (g, WIDE, gh))

    core = lax.rem(c, 2)
    sibling = device(dc=C + 1 - 2 * core)

    def next_turn(n):
        pl.semaphore_signal(turn.at[n], inc=1, device_id=sibling, device_id_type=pl.DeviceIdType.MESH)

    def z_copy(n, d):
        src, width, dst = by_head[n]
        to = lax.rem(z + d, Z)
        return remote(src.at[:, at(to, width)], dst.at[z], z_send.at[n, d], z_recv.at[n, d], device(dz=d))

    def keys_copy(e, d):
        to, head = lax.rem(c + e, C), lax.rem(z + d, Z)
        return remote(
            k.at[at(to, ROWS), at(head, HEAD_SIZE)], tab_k.at[y * SHARE + c * Z + z],
            d_sem.at[0], d_sem.at[1], device(dc=e, dz=d),
        )

    def keys_all():
        all_but_one = tab_k.at[pl.ds(0, SHARE - 1)]
        return remote(all_but_one, all_but_one, d_sem.at[0], d_sem.at[1], device(dc=1))

    for d in range(Z):
        for e in range(C):
            if d or e:
                keys_copy(e, d).start()
    for n in range(1, 4):
        for d in range(1, Z):
            z_copy(n, d).start()
    tab_k[y * SHARE + c * Z + z] = k[at(c, ROWS), at(z, HEAD_SIZE)]
    vz[z] = v[:, at(z, HEAD_SIZE)]
    own_q = pltpu.make_async_copy(q.at[:, at(z, WIDE)], qh.at[z], own_sem.at[3])
    own_g = pltpu.make_async_copy(g.at[:, at(z, WIDE)], gh.at[z], own_sem.at[4])
    own_q.start()
    own_g.start()

    mine = at(y * C + c, Z)

    def s_copy(n, d):
        to = lax.rem(c + d, C)
        if n:
            src, dst = vz.at[:, at(to, ROWS)], tab_v.at[mine]
        else:
            src, dst = tab_k.at[at(y * C + to, Z)], kz.at[:, at(c, ROWS)]
        return remote(src, dst, s_send.at[n, d], s_recv.at[n, d], device(dc=d))

    def ring(n, s, way, half):
        tab = (tab_k, tab_v)[n]
        owner = lax.rem(y - way * s + Y, Y)
        part = tab.at[at(owner * PARTS + half, PIECE)]
        lane = 0 if way > 0 else 1
        return remote(part, part, ag_send.at[n, s, lane, half], ag_recv.at[n, s, lane, half], device(dy=way))

    ring_order = []
    for n in range(PARTS):
        ring_order += [(1, n), (-1, (n + PARTS // 2) % PARTS)]

    def hops(way, half):
        return STEPS if (way, half) in ring_order[:PARTS] else STEPS - 1

    def ring_sent(s, way, half):
        return y != Y - 1 if way > 0 else lax.rem(y + s, Y) < hops(way, half)

    def ring_received(s, way, half):
        return y != 0 if way > 0 else lax.rem(y + s + 1, Y) < hops(way, half)

    def ring_start(n, s, way, half):
        pl.when(ring_sent(s, way, half))(lambda: ring(n, s, way, half).start())

    def ring_wait(n, s, way, half):
        pl.when(ring_received(s, way, half))(lambda: ring(n, s, way, half).wait_recv())

    def ring_first(n):
        for way, half in ring_order:
            ring_start(n, 0, way, half)

    def ring_next(n, s):
        for way, half in ring_order[: PARTS if s == STEPS - 1 else 2 * PARTS]:
            ring_wait(n, s - 1, way, half)
            ring_start(n, s, way, half)

    def ring_last(n):
        for way, half in ring_order[PARTS:]:
            ring_wait(n, STEPS - 2, way, half)
        for way, half in ring_order[:PARTS]:
            ring_wait(n, STEPS - 1, way, half)

    def chosen_row():
        two = sel_rows[:, at(lax.div(y, 2), 2 * SHARE)]
        turned = pltpu.roll(two, SHARE, 1)
        low = jnp.where(lax.rem(y, 2) == 0, two, turned)
        high = jnp.where(lax.rem(y, 2) == 0, turned, two)
        lane = lax.broadcasted_iota(jnp.int32, (1, 2 * SHARE), 1)
        return jnp.concatenate(
            [
                jnp.where(lane < SHARE, low[j : j + 1], high[j + 1 : j + 2])
                for j in range(0, CHOSEN_BLOCKS, 2)
            ],
            axis=1,
        )

    def pack(tab, out, own, first, count):
        for d in range(C):
            to = lax.rem(c + d, C)

            @pl.loop(first, first + count)
            def _(i):
                for j in range(OTHERS):
                    rows = tab[sel[1 + j, y * SHARE + to * Z + i]]
                    if d:
                        out[d, i * OTHERS + j] = rows
                    else:
                        own[c, i * OTHERS + j] = rows

    def k_copy(d):
        return remote(out_k.at[d], in_k.at[c], k_send.at[d], k_recv.at[d], device(dc=d))

    part = UNITS // SPLITS

    def v_copy(d, n):
        span = pl.ds(n * part, part)
        return remote(out_v.at[d, span], in_v.at[c, span], v_send.at[d, n], v_recv.at[d, n], device(dc=d))

    def rv_copy(d, n):
        to = lax.rem(c + d, C)
        return remote(
            dv_out.at[to, pl.ds(n * part, part)], ret_v.at[pl.ds(c * UNITS + n * part, part)],
            rv_send.at[d, n], rv_recv.at[d, n], device(dc=d),
        )

    def rk_copy(d):
        to = lax.rem(c + d, C)
        return remote(dk_out.at[to], ret_k.at[at(c, UNITS)], rk_send.at[d], rk_recv.at[d], device(dc=d))

    keys_all().wait_recv()

    @pl.when(core == 0)
    def _():
        ring_first(0)
        ring_next(0, 1)

    for d in range(1, C):
        s_copy(0, d).start()
    kz[:, at(c, ROWS)] = tab_k[mine]
    for d in range(1, Z):
        z_copy(1, d).wait_recv()
    for d in range(1, C):
        s_copy(1, d).start()
    tab_v[mine] = vz[:, at(c, ROWS)]

    @pl.when(core == 1)
    def _():
        pl.semaphore_wait(turn.at[0], 1)
        ring_first(0)
        ring_next(0, 1)

    for s in range(2, STEPS):
        ring_next(0, s)
        if s == TURN_STEP:
            next_turn(core)
    for d in range(1, C):
        s_copy(1, d).wait_recv()
    ring_last(0)
    pack(tab_k, out_k, in_k, 0, Z)
    for d in range(1, C):
        k_copy(d).start()
    pl.semaphore_wait(turn.at[1 + core], 1)
    ring_first(1)
    for s in range(1, STEPS):
        ring_next(1, s)
        if s == TURN_STEP:

            @pl.when(core == 0)
            def _():
                next_turn(2)

    order_requests(chosen_row(), order_v)
    to_scalars = pltpu.make_async_copy(order_v, order, own_sem.at[2])
    to_scalars.start()
    to_scalars.wait()
    ring_last(1)

    for n in range(SPLITS):
        pack(tab_v, out_v, in_v, n * PER_SPLIT, PER_SPLIT)
        for d in range(1, C):
            v_copy(d, n).start()

    own_q.wait()
    own_g.wait()
    for n in (2, 3):
        for d in range(1, Z):
            z_copy(n, d).wait_recv()
    for d in range(1, C):
        s_copy(0, d).wait_recv()
        k_copy(d).wait_recv()

    @pl.loop(0, SPLITS)
    def _(n):
        @pl.loop(0, PER_SPLIT)
        def _(m):
            i = n * PER_SPLIT + m
            block = y * SHARE + c * Z + i
            probs_block(i, block, lambda j: sel[j, block], qh, gh, kz, in_k, dv_own, dv_out, probs)

        for d in range(1, C):
            rv_copy(d, n).start()

    @pl.loop(0, SPLITS)
    def _(n):
        for d in range(1, C):
            v_copy(d, n).wait_recv()

        @pl.loop(0, PER_SPLIT)
        def _(m):
            i = n * PER_SPLIT + m
            scores_block(i, qh, gh, kz, vz, in_k, in_v, dq, dk_own, dk_out, probs, dscores)

    own_v = pltpu.make_async_copy(dv_out.at[c], ret_v.at[at(c, UNITS)], own_sem.at[0])
    own_k = pltpu.make_async_copy(dk_out.at[c], ret_k.at[at(c, UNITS)], own_sem.at[1])
    own_v.start()
    own_k.start()
    own_v.wait()
    own_k.wait()

    nothing = jnp.zeros((ROWS, HEAD_SIZE), jnp.float32)
    runs[REQUESTS] = nothing

    def run_sums(ret):
        def add(p, total):
            total = ret[order[0, p]].astype(jnp.float32) + jnp.where(order[1, p] == 1, total, 0.0)
            runs[p] = total
            return total

        lax.fori_loop(0, REQUESTS, add, nothing, unroll=8)

    def rs_copy(n, s, way, half):
        lane = 0 if way > 0 else 1
        return remote(
            rs_out.at[n, lane, s, half], rs_in.at[n, lane, s, half],
            rs_send.at[n, lane, s, half], rs_recv.at[n, lane, s, half], device(dy=way),
        )

    def rs_sent(s, way, half):
        if way > 0:
            return lax.rem(y + STEPS - s, Y) < hops(way, half)
        return y >= STEPS - s

    def rs_step(n, s, way, half, arrived):
        lane = 0 if way > 0 else 1
        owner = lax.rem(y + way * (STEPS - s) + Y, Y)

        @pl.when(rs_sent(s, way, half))
        def _():
            if arrived and way > 0:
                rs_copy(n, s - 1, way, half).wait_recv()
            elif arrived:
                pl.when(y != Y - 1)(lambda: rs_copy(n, s - 1, way, half).wait_recv())

            @pl.loop(0, PIECE, unroll=8)
            def _(t):
                total = runs[order[2, owner * SHARE + half * PIECE + t]]
                if arrived:
                    before = rs_in[n, lane, s - 1, half, t].astype(jnp.float32)
                    total += before if way > 0 else jnp.where(y != Y - 1, before, 0.0)
                rs_out[n, lane, s, half, t] = total.astype(jnp.bfloat16)

            if s < STEPS - 1:
                rs_copy(n, s, way, half).start()
            else:
                for m in range(C // PARTS):
                    last_copy(n, way, half, m).start()

    def last_copy(n, way, half, m):
        lane = 0 if way > 0 else 1
        to = half * (C // PARTS) + m
        e = lax.rem(to - c + C, C)
        return remote(
            rs_out.at[n, lane, STEPS - 1, half, pl.ds(m * Z, Z)], fin_in.at[n, lane, :, at(c, ROWS)],
            l_send.at[n, lane, e], l_recv.at[n, lane, e], (lax.rem(y + way + Y, Y), to, z),
        )

    def u_copy(n, d):
        to = lax.rem(c + d, C)
        return remote(
            fin_out.at[n, at(to, Z)], fin_in.at[n, 2, :, at(c, ROWS)], u_send.at[n, d], u_recv.at[n, d], device(dc=d)
        )

    def reduce_own(n):
        @pl.loop(0, SHARE, unroll=8)
        def _(t):
            fin_out[n, t] = runs[order[2, y * SHARE + t]].astype(jnp.bfloat16)

        for d in range(1, C):
            u_copy(n, d).start()
        fin_in[n, 2, :, at(c, ROWS)] = fin_out[n, at(c, Z)]

    def reduce_first(n):
        for way, half in ring_order[:PARTS]:
            rs_step(n, 0, way, half, False)
        for way, half in ring_order[PARTS:]:
            rs_step(n, 1, way, half, False)

    def reduce_next(n):
        for way, half in ring_order[:PARTS]:
            rs_step(n, 1, way, half, True)
        for s in range(2, STEPS):
            for way, half in ring_order[PARTS:] + ring_order[:PARTS]:
                rs_step(n, s, way, half, True)

    for n in range(SPLITS):
        for d in range(1, C):
            rv_copy(d, n).wait_recv()
    for d in range(1, C):
        rk_copy(d).start()
    run_sums(ret_v)
    reduce_first(1)
    reduce_own(1)
    reduce_next(1)
    for d in range(1, C):
        rk_copy(d).wait_recv()
    run_sums(ret_k)
    reduce_first(0)
    reduce_own(0)
    reduce_next(0)
    from_below = y < jnp.where(c < C // 2, hops(1, 0), hops(1, PARTS - 1))
    from_above = y != Y - 1
    for n, own, out in ((1, dv_own, dv), (0, dk_own, dk)):
        for d in range(1, C):
            u_copy(n, d).wait_recv()
        for way, received in ((1, from_below), (-1, from_above)):

            @pl.when(received)
            def _():
                for half in range(PARTS):
                    for m in range(C // PARTS):
                        last_copy(n, way, half, m).wait_recv()

        for i in range(Z):
            total = own[i] + fin_in[n, 2, i].astype(jnp.float32)
            total += jnp.where(from_below, fin_in[n, 0, i].astype(jnp.float32), 0.0)
            total += jnp.where(from_above, fin_in[n, 1, i].astype(jnp.float32), 0.0)
            out[i] = total.astype(jnp.bfloat16)

    keys_all().wait_send()
    for d in range(1, Z):
        for n in range(1, 4):
            z_copy(n, d).wait_send()
    for d in range(1, C):
        for n in range(2):
            s_copy(n, d).wait_send()
            u_copy(n, d).wait_send()
        k_copy(d).wait_send()
        rk_copy(d).wait_send()
        for n in range(SPLITS):
            v_copy(d, n).wait_send()
            rv_copy(d, n).wait_send()
    for n in range(2):
        for s in range(STEPS):
            for way, half in ring_order[: PARTS if s == STEPS - 1 else 2 * PARTS]:
                pl.when(ring_sent(s, way, half))(lambda: ring(n, s, way, half).wait_send())
            for way, half in ring_order[: PARTS if s == 0 else 2 * PARTS]:

                @pl.when(rs_sent(s, way, half))
                def _():
                    if s < STEPS - 1:
                        rs_copy(n, s, way, half).wait_send()
                    else:
                        for m in range(C // PARTS):
                            last_copy(n, way, half, m).wait_send()


def whole(sel, k, v, q, g):
    vmem = pl.BlockSpec(memory_space=pltpu.VMEM)
    bf16 = lambda *shape: pltpu.VMEM(shape, jnp.bfloat16)
    f32 = lambda *shape: pltpu.VMEM(shape, jnp.float32)
    dma = lambda *shape: pltpu.SemaphoreType.DMA(shape)
    units = (C, UNITS, ROWS, HEAD_SIZE)
    table = (BLOCKS, ROWS, HEAD_SIZE)
    heads = (Z, BLOCK_TOKENS, HEAD_SIZE)
    steps = (2, 2, STEPS, PARTS, PIECE, ROWS, HEAD_SIZE)
    return pl.pallas_call(
        whole_kernel,
        out_shape=(
            jax.ShapeDtypeStruct((Z * BLOCK_TOKENS, WIDE), jnp.bfloat16),
            jax.ShapeDtypeStruct(heads, jnp.bfloat16),
            jax.ShapeDtypeStruct(heads, jnp.bfloat16),
        ),
        in_specs=[pl.BlockSpec(memory_space=pltpu.SMEM)] + [vmem] * 3 + [pl.BlockSpec(memory_space=pl.ANY)] * 2,
        out_specs=[vmem] * 3,
        scratch_shapes=[bf16(*heads)] * 2
        + [bf16(Z, BLOCK_TOKENS, WIDE)] * 2
        + [bf16(*table)] * 2
        + [bf16(*units)] * 6
        + [bf16(REQUESTS, ROWS, HEAD_SIZE)] * 2
        + [bf16(Z, KEYS, WIDE), bf16(KEYS, WIDE)]
        + [f32(*heads)] * 2
        + [f32(REQUESTS + 8, ROWS, HEAD_SIZE)]
        + [bf16(*steps)] * 2
        + [bf16(2, SHARE, ROWS, HEAD_SIZE)]
        + [bf16(2, 3, *heads)]
        + [pltpu.VMEM((8, SLOTS), jnp.int32), pltpu.SMEM((8, SLOTS), jnp.int32)]
        + [dma(4, Z)] * 2
        + [dma(2, C)] * 2
        + [dma(2, STEPS, 2, PARTS)] * 2
        + [dma(C)] * 2
        + [dma(C, SPLITS)] * 4
        + [dma(C)] * 2
        + [dma(2, 2, STEPS, PARTS)] * 2
        + [dma(2, C)] * 2
        + [dma(5)]
        + [dma(2)]
        + [dma(2, 2, C)] * 2
        + [pltpu.SemaphoreType.REGULAR((3,))],
        compiler_params=pltpu.CompilerParams(
            vmem_limit_bytes=VMEM, collective_id=0, has_side_effects=True
        ),
        name="whole",
    )(sel, sel, k, v, q, g)


def finish_kernel(dq, dk, dv, dq_out, dk_out, dv_out):
    dq_out[...] = dq[...]
    dk_out[...] = dk[...]
    dv_out[...] = dv[...]


def finish(*arrays):
    vmem = pl.BlockSpec(memory_space=pltpu.VMEM)
    return pl.pallas_call(
        finish_kernel,
        out_shape=tuple(jax.ShapeDtypeStruct(a.shape, a.dtype) for a in arrays),
        in_specs=[vmem] * len(arrays),
        out_specs=[vmem] * len(arrays),
        compiler_params=pltpu.CompilerParams(vmem_limit_bytes=VMEM),
        name="finish",
    )(*arrays)


def body(query, keys, values, output_cotangent, select):
    by_slot = select.reshape(BLOCKS, CHOSEN_BLOCKS).T
    dq, dk, dv = finish(*whole(by_slot, keys, values, query, output_cotangent))
    rows = (Z * BLOCK_TOKENS, HEAD_SIZE)
    return dq, dk.reshape(rows), dv.reshape(rows)


def solution(mesh):
    groups = mesh.shape["grp"]
    grid = jax.sharding.Mesh(
        mesh.devices.reshape(-1, STRIPES, groups), ("y", "xc", "grp")
    )
    rows = ("y", "xc")
    in_specs = (P(rows + ("grp",), None),) * 4 + (P(None, "grp", None),)
    out_specs = (P(rows, "grp"),) * 3
    return jax.shard_map(
        body, mesh=grid, in_specs=in_specs, out_specs=out_specs, check_vma=False
    )
```

```python
import functools

import jax
import jax.numpy as jnp
from jax import lax
from jax.experimental import pallas as pl
from jax.experimental.pallas import tpu as pltpu
from jax.sharding import PartitionSpec as P

HEAD_SIZE = 128
QUERY_HEADS = 32
KEY_HEADS = 8
BLOCK_TOKENS = 128
CHOSEN_BLOCKS = 8
GROUP = QUERY_HEADS // KEY_HEADS
STRIPES = 8
ROWS = BLOCK_TOKENS // STRIPES
KEYS = CHOSEN_BLOCKS * BLOCK_TOKENS
FACTOR = HEAD_SIZE ** (-0.5)
VMEM = 56 * 1024 * 1024


def nt(a, b):
    return lax.dot_general(a, b, (((1,), (1,)), ((), ())), preferred_element_type=jnp.float32)


def nn(a, b):
    return jnp.dot(a, b, preferred_element_type=jnp.float32)


Y, C, Z = 8, 8, 8
OTHERS = CHOSEN_BLOCKS - 1
OTHER_KEYS = OTHERS * BLOCK_TOKENS
UNITS = Z * OTHERS
REQUESTS = C * UNITS
SLOTS = C * Z * CHOSEN_BLOCKS
SHARE = C * Z
BLOCKS = Y * SHARE
PARTS = 4
PIECE = SHARE // PARTS
STEPS = 4
TURN_STEP = 2
SPLITS = 4
PER_SPLIT = Z // SPLITS
WIDE = GROUP * HEAD_SIZE
OTHERS_SHAPE = (STRIPES, OTHERS, ROWS, HEAD_SIZE)


def at(index, size):
    return pl.ds(pl.multiple_of(index * size, size), size)


def probs_block(i, own, sel_at, q_ref, g_ref, kz, k_ref, dv_own, dv_ref, probs):
    units = pl.ds(i * OTHERS, OTHERS)
    keys = jnp.concatenate([kz[i], k_ref[:, units].reshape(OTHER_KEYS, HEAD_SIZE)], 0)
    row = lax.broadcasted_iota(jnp.int32, (BLOCK_TOKENS, BLOCK_TOKENS), 0)
    token = lax.broadcasted_iota(jnp.int32, (BLOCK_TOKENS, BLOCK_TOKENS), 1)
    own_bias = jnp.where(row <= token, 0.0, -jnp.inf).astype(jnp.float32)
    other_bias = jnp.stack(
        [
            jnp.full(
                (STRIPES, ROWS, BLOCK_TOKENS), jnp.where(sel_at(j) < own, 0.0, -jnp.inf), jnp.float32
            )
            for j in range(1, CHOSEN_BLOCKS)
        ],
        axis=1,
    ).reshape(OTHER_KEYS, BLOCK_TOKENS)
    bias = jnp.concatenate([own_bias, other_bias], 0)
    for h in range(GROUP):
        cols = pl.ds(h * HEAD_SIZE, HEAD_SIZE)
        scores = nt(keys, q_ref[i, :, cols]) * FACTOR + bias
        highest = jnp.max(scores, axis=0, keepdims=True)
        weights = jnp.exp(scores - highest)
        prob = weights * (1.0 / jnp.sum(weights, axis=0, keepdims=True))
        probs[i, :, cols] = prob.astype(jnp.bfloat16)
    dv = nn(probs[i], by_head_rows(g_ref, i))
    dv_own[i] = dv[:BLOCK_TOKENS]
    dv_ref[:, units] = dv[BLOCK_TOKENS:].astype(jnp.bfloat16).reshape(OTHERS_SHAPE)


def by_head_rows(ref, i):
    return jnp.concatenate([ref[i, :, h * HEAD_SIZE : (h + 1) * HEAD_SIZE] for h in range(GROUP)], 0)


def scores_block(i, q_ref, g_ref, kz, vz, k_ref, v_ref, dq_ref, dk_own, dk_ref, probs, dscores):
    units = pl.ds(i * OTHERS, OTHERS)
    keys = jnp.concatenate([kz[i], k_ref[:, units].reshape(OTHER_KEYS, HEAD_SIZE)], 0)
    vals = jnp.concatenate([vz[i], v_ref[:, units].reshape(OTHER_KEYS, HEAD_SIZE)], 0)
    for h in range(GROUP):
        cols = pl.ds(h * HEAD_SIZE, HEAD_SIZE)
        prob = probs[i, :, cols].astype(jnp.float32)
        dprobs = nt(vals, g_ref[i, :, cols])
        delta = jnp.sum(prob * dprobs, axis=0, keepdims=True)
        dscores[:, cols] = (prob * (dprobs - delta)).astype(jnp.bfloat16)
    dk = nn(dscores[...], by_head_rows(q_ref, i)) * FACTOR
    dk_own[i] = dk[:BLOCK_TOKENS]
    dk_ref[:, units] = dk[BLOCK_TOKENS:].astype(jnp.bfloat16).reshape(OTHERS_SHAPE)
    dq_t = nn(keys.T, dscores[...]) * FACTOR
    for h in range(GROUP):
        cols = pl.ds(h * HEAD_SIZE, HEAD_SIZE)
        dq_ref[at(i, BLOCK_TOKENS), cols] = (
            dq_t[:, h * HEAD_SIZE : (h + 1) * HEAD_SIZE].T.astype(jnp.bfloat16)
        )


def order_requests(sel_row, order):
    lane = lax.broadcasted_iota(jnp.int32, (1, SLOTS), 1)
    key = jnp.where(lane < SHARE, BLOCKS * SLOTS, sel_row * SLOTS + lane)

    def column(x):
        return jnp.broadcast_to(x, (128, SLOTS)).T[:, :1]

    index = lax.broadcasted_iota(jnp.int32, (SLOTS, 1), 0)
    valid = index >= SHARE
    chosen = column(sel_row)
    rank = jnp.sum((key < column(key)).astype(jnp.int32), axis=1, keepdims=True)
    rank = jnp.where(valid, rank, -2)
    place = lax.rem(index, SHARE) * OTHERS + lax.div(index, SHARE) - 1

    def pick(mask, value):
        return jnp.sum(jnp.where(mask, value, 0), axis=0, keepdims=True)

    here = pick(rank == lane, chosen + 1)
    before = pick(rank + 1 == lane, chosen + 1)
    upto = pick(valid & (chosen <= lane), 1)
    count = pick(valid & (chosen == lane), 1)
    order[...] = jnp.zeros_like(order)
    order[0:1, :] = pick(rank == lane, place)
    order[1:2, :] = (here == before).astype(jnp.int32)
    order[2:3, :] = jnp.where(count > 0, upto - 1, REQUESTS)


def whole_kernel(
    sel, sel_rows, k, v, q, g, dq, dk, dv,
    kz, vz, qh, gh, tab_k, tab_v, out_k, out_v, in_k, in_v, dk_out, dv_out, ret_k, ret_v, probs, dscores,
    dk_own, dv_own, runs, rs_out, rs_in, fin_out, fin_in, order_v, order,
    z_send, z_recv, s_send, s_recv, ag_send, ag_recv, k_send, k_recv, v_send, v_recv,
    rv_send, rv_recv, rk_send, rk_recv, rs_send, rs_recv, u_send, u_recv, own_sem, d_sem, l_send, l_recv, turn,
):
    y, c, z = lax.axis_index("y"), lax.axis_index("xc"), lax.axis_index("grp")

    def device(dy=0, dc=0, dz=0):
        return (lax.rem(y + dy + Y, Y), lax.rem(c + dc, C), lax.rem(z + dz, Z))

    def remote(src, dst, send, recv, target):
        return pltpu.make_async_remote_copy(
            src_ref=src, dst_ref=dst, send_sem=send, recv_sem=recv,
            device_id=target, device_id_type=pl.DeviceIdType.MESH,
        )

    barrier = pltpu.get_barrier_semaphore()
    partners = [device(dc=e, dz=d) for e in range(C) for d in range(Z) if e or d]
    partners += [device(dy=way, dc=e) for way in (1, -1) for e in range(C)]
    for p in partners:
        pl.semaphore_signal(barrier, inc=1, device_id=p, device_id_type=pl.DeviceIdType.MESH)
    pl.semaphore_wait(barrier, len(partners))

    by_head = (None, (v, HEAD_SIZE, vz), (q, WIDE, qh), (g, WIDE, gh))

    core = lax.rem(c, 2)
    sibling = device(dc=C + 1 - 2 * core)

    def next_turn(n):
        pl.semaphore_signal(turn.at[n], inc=1, device_id=sibling, device_id_type=pl.DeviceIdType.MESH)

    def z_copy(n, d):
        src, width, dst = by_head[n]
        to = lax.rem(z + d, Z)
        return remote(src.at[:, at(to, width)], dst.at[z], z_send.at[n, d], z_recv.at[n, d], device(dz=d))

    def keys_copy(e, d):
        to, head = lax.rem(c + e, C), lax.rem(z + d, Z)
        return remote(
            k.at[at(to, ROWS), at(head, HEAD_SIZE)], tab_k.at[y * SHARE + c * Z + z],
            d_sem.at[0], d_sem.at[1], device(dc=e, dz=d),
        )

    def keys_all():
        all_but_one = tab_k.at[pl.ds(0, SHARE - 1)]
        return remote(all_but_one, all_but_one, d_sem.at[0], d_sem.at[1], device(dc=1))

    for d in range(Z):
        for e in range(C):
            if d or e:
                keys_copy(e, d).start()
    for d in range(1, Z):
        z_copy(1, d).start()
    tab_k[y * SHARE + c * Z + z] = k[at(c, ROWS), at(z, HEAD_SIZE)]
    vz[z] = v[:, at(z, HEAD_SIZE)]
    own_q = pltpu.make_async_copy(q.at[:, at(z, WIDE)], qh.at[z], own_sem.at[3])
    own_g = pltpu.make_async_copy(g.at[:, at(z, WIDE)], gh.at[z], own_sem.at[4])
    own_q.start()
    own_g.start()

    mine = at(y * C + c, Z)

    def s_copy(n, d):
        to = lax.rem(c + d, C)
        if n:
            src, dst = vz.at[:, at(to, ROWS)], tab_v.at[mine]
        else:
            src, dst = tab_k.at[at(y * C + to, Z)], kz.at[:, at(c, ROWS)]
        return remote(src, dst, s_send.at[n, d], s_recv.at[n, d], device(dc=d))

    def ring(n, s, way, half):
        tab = (tab_k, tab_v)[n]
        owner = lax.rem(y - way * s + Y, Y)
        part = tab.at[at(owner * PARTS + half, PIECE)]
        lane = 0 if way > 0 else 1
        return remote(part, part, ag_send.at[n, s, lane, half], ag_recv.at[n, s, lane, half], device(dy=way))

    ring_order = []
    for n in range(PARTS):
        ring_order += [(1, n), (-1, (n + PARTS // 2) % PARTS)]

    def hops(way, half):
        return STEPS if (way, half) in ring_order[:PARTS] else STEPS - 1

    def ring_sent(s, way, half):
        return y != Y - 1 if way > 0 else lax.rem(y + s, Y) < hops(way, half)

    def ring_received(s, way, half):
        return y != 0 if way > 0 else lax.rem(y + s + 1, Y) < hops(way, half)

    def ring_start(n, s, way, half):
        pl.when(ring_sent(s, way, half))(lambda: ring(n, s, way, half).start())

    def ring_wait(n, s, way, half):
        pl.when(ring_received(s, way, half))(lambda: ring(n, s, way, half).wait_recv())

    def ring_first(n):
        for way, half in ring_order:
            ring_start(n, 0, way, half)

    def ring_next(n, s):
        for way, half in ring_order[: PARTS if s == STEPS - 1 else 2 * PARTS]:
            ring_wait(n, s - 1, way, half)
            ring_start(n, s, way, half)

    def ring_last(n):
        for way, half in ring_order[PARTS:]:
            ring_wait(n, STEPS - 2, way, half)
        for way, half in ring_order[:PARTS]:
            ring_wait(n, STEPS - 1, way, half)

    def chosen_row():
        two = sel_rows[:, at(lax.div(y, 2), 2 * SHARE)]
        turned = pltpu.roll(two, SHARE, 1)
        low = jnp.where(lax.rem(y, 2) == 0, two, turned)
        high = jnp.where(lax.rem(y, 2) == 0, turned, two)
        lane = lax.broadcasted_iota(jnp.int32, (1, 2 * SHARE), 1)
        return jnp.concatenate(
            [
                jnp.where(lane < SHARE, low[j : j + 1], high[j + 1 : j + 2])
                for j in range(0, CHOSEN_BLOCKS, 2)
            ],
            axis=1,
        )

    def pack(tab, out, own, first, count):
        for d in range(C):
            to = lax.rem(c + d, C)

            @pl.loop(first, first + count)
            def _(i):
                for j in range(OTHERS):
                    block = sel[1 + j, y * SHARE + to * Z + i]
                    rows = jnp.where(block < (y + 1) * SHARE, tab[block], 0.0).astype(tab.dtype)
                    if d:
                        out[d, i * OTHERS + j] = rows
                    else:
                        own[c, i * OTHERS + j] = rows

    def k_copy(d):
        return remote(out_k.at[d], in_k.at[c], k_send.at[d], k_recv.at[d], device(dc=d))

    part = UNITS // SPLITS

    def v_copy(d, n):
        span = pl.ds(n * part, part)
        return remote(out_v.at[d, span], in_v.at[c, span], v_send.at[d, n], v_recv.at[d, n], device(dc=d))

    def rv_copy(d, n):
        to = lax.rem(c + d, C)
        return remote(
            dv_out.at[to, pl.ds(n * part, part)], ret_v.at[pl.ds(c * UNITS + n * part, part)],
            rv_send.at[d, n], rv_recv.at[d, n], device(dc=d),
        )

    def rk_copy(d):
        to = lax.rem(c + d, C)
        return remote(dk_out.at[to], ret_k.at[at(c, UNITS)], rk_send.at[d], rk_recv.at[d], device(dc=d))

    keys_all().wait_recv()

    @pl.when(core == 0)
    def _():
        ring_first(0)
        ring_next(0, 1)

    for n in (2, 3):
        for d in range(1, Z):
            z_copy(n, d).start()
    for d in range(1, C):
        s_copy(0, d).start()
    kz[:, at(c, ROWS)] = tab_k[mine]
    for d in range(1, Z):
        z_copy(1, d).wait_recv()
    for d in range(1, C):
        s_copy(1, d).start()
    tab_v[mine] = vz[:, at(c, ROWS)]

    @pl.when(core == 1)
    def _():
        pl.semaphore_wait(turn.at[0], 1)
        ring_first(0)
        ring_next(0, 1)

    for s in range(2, STEPS):
        ring_next(0, s)
        if s == TURN_STEP:
            next_turn(core)
    for d in range(1, C):
        s_copy(1, d).wait_recv()
    ring_last(0)
    pack(tab_k, out_k, in_k, 0, Z)
    for d in range(1, C):
        k_copy(d).start()
    pl.semaphore_wait(turn.at[1 + core], 1)
    ring_first(1)
    for s in range(1, STEPS):
        ring_next(1, s)
        if s == TURN_STEP:

            @pl.when(core == 0)
            def _():
                next_turn(2)

    order_requests(chosen_row(), order_v)
    to_scalars = pltpu.make_async_copy(order_v, order, own_sem.at[2])
    to_scalars.start()
    to_scalars.wait()
    ring_last(1)

    for n in range(SPLITS):
        pack(tab_v, out_v, in_v, n * PER_SPLIT, PER_SPLIT)
        for d in range(1, C):
            v_copy(d, n).start()

    own_q.wait()
    own_g.wait()
    for n in (2, 3):
        for d in range(1, Z):
            z_copy(n, d).wait_recv()
    for d in range(1, C):
        s_copy(0, d).wait_recv()
        k_copy(d).wait_recv()

    @pl.loop(0, SPLITS)
    def _(n):
        @pl.loop(0, PER_SPLIT)
        def _(m):
            i = n * PER_SPLIT + m
            block = y * SHARE + c * Z + i
            probs_block(i, block, lambda j: sel[j, block], qh, gh, kz, in_k, dv_own, dv_out, probs)

        for d in range(1, C):
            rv_copy(d, n).start()

    @pl.loop(0, SPLITS)
    def _(n):
        for d in range(1, C):
            v_copy(d, n).wait_recv()

        @pl.loop(0, PER_SPLIT)
        def _(m):
            i = n * PER_SPLIT + m
            scores_block(i, qh, gh, kz, vz, in_k, in_v, dq, dk_own, dk_out, probs, dscores)

    own_v = pltpu.make_async_copy(dv_out.at[c], ret_v.at[at(c, UNITS)], own_sem.at[0])
    own_k = pltpu.make_async_copy(dk_out.at[c], ret_k.at[at(c, UNITS)], own_sem.at[1])
    own_v.start()
    own_k.start()
    own_v.wait()
    own_k.wait()

    nothing = jnp.zeros((ROWS, HEAD_SIZE), jnp.float32)
    runs[REQUESTS] = nothing

    def run_sums(ret):
        def add(p, total):
            total = ret[order[0, p]].astype(jnp.float32) + jnp.where(order[1, p] == 1, total, 0.0)
            runs[p] = total
            return total

        lax.fori_loop(0, REQUESTS, add, nothing, unroll=8)

    def rs_copy(n, s, way, half):
        lane = 0 if way > 0 else 1
        return remote(
            rs_out.at[n, lane, s, half], rs_in.at[n, lane, s, half],
            rs_send.at[n, lane, s, half], rs_recv.at[n, lane, s, half], device(dy=way),
        )

    def rs_sent(s, way, half):
        if way > 0:
            return lax.rem(y + STEPS - s, Y) < hops(way, half)
        return y >= STEPS - s

    def rs_step(n, s, way, half, arrived):
        lane = 0 if way > 0 else 1
        owner = lax.rem(y + way * (STEPS - s) + Y, Y)

        @pl.when(rs_sent(s, way, half))
        def _():
            if arrived and way > 0:
                rs_copy(n, s - 1, way, half).wait_recv()
            elif arrived:
                pl.when(y != Y - 1)(lambda: rs_copy(n, s - 1, way, half).wait_recv())

            @pl.loop(0, PIECE, unroll=8)
            def _(t):
                total = runs[order[2, owner * SHARE + half * PIECE + t]]
                if arrived:
                    before = rs_in[n, lane, s - 1, half, t].astype(jnp.float32)
                    total += before if way > 0 else jnp.where(y != Y - 1, before, 0.0)
                rs_out[n, lane, s, half, t] = total.astype(jnp.bfloat16)

            if s < STEPS - 1:
                rs_copy(n, s, way, half).start()
            else:
                for m in range(C // PARTS):
                    last_copy(n, way, half, m).start()

    def last_copy(n, way, half, m):
        lane = 0 if way > 0 else 1
        to = half * (C // PARTS) + m
        e = lax.rem(to - c + C, C)
        return remote(
            rs_out.at[n, lane, STEPS - 1, half, pl.ds(m * Z, Z)], fin_in.at[n, lane, :, at(c, ROWS)],
            l_send.at[n, lane, e], l_recv.at[n, lane, e], (lax.rem(y + way + Y, Y), to, z),
        )

    def u_copy(n, d):
        to = lax.rem(c + d, C)
        return remote(
            fin_out.at[n, at(to, Z)], fin_in.at[n, 2, :, at(c, ROWS)], u_send.at[n, d], u_recv.at[n, d], device(dc=d)
        )

    def reduce_own(n):
        @pl.loop(0, SHARE, unroll=8)
        def _(t):
            fin_out[n, t] = runs[order[2, y * SHARE + t]].astype(jnp.bfloat16)

        for d in range(1, C):
            u_copy(n, d).start()
        fin_in[n, 2, :, at(c, ROWS)] = fin_out[n, at(c, Z)]

    def reduce_first(n):
        for way, half in ring_order[:PARTS]:
            rs_step(n, 0, way, half, False)
        for way, half in ring_order[PARTS:]:
            rs_step(n, 1, way, half, False)

    def reduce_next(n):
        for way, half in ring_order[:PARTS]:
            rs_step(n, 1, way, half, True)
        for s in range(2, STEPS):
            for way, half in ring_order[PARTS:] + ring_order[:PARTS]:
                rs_step(n, s, way, half, True)

    for n in range(SPLITS):
        for d in range(1, C):
            rv_copy(d, n).wait_recv()
    for d in range(1, C):
        rk_copy(d).start()
    run_sums(ret_v)
    reduce_first(1)
    reduce_own(1)
    reduce_next(1)
    for d in range(1, C):
        rk_copy(d).wait_recv()
    run_sums(ret_k)
    reduce_first(0)
    reduce_own(0)
    reduce_next(0)
    from_below = y < jnp.where(c < C // 2, hops(1, 0), hops(1, PARTS - 1))
    from_above = y != Y - 1
    for n, own, out in ((1, dv_own, dv), (0, dk_own, dk)):
        for d in range(1, C):
            u_copy(n, d).wait_recv()
        for way, received in ((1, from_below), (-1, from_above)):

            @pl.when(received)
            def _():
                for half in range(PARTS):
                    for m in range(C // PARTS):
                        last_copy(n, way, half, m).wait_recv()

        for i in range(Z):
            total = own[i] + fin_in[n, 2, i].astype(jnp.float32)
            total += jnp.where(from_below, fin_in[n, 0, i].astype(jnp.float32), 0.0)
            total += jnp.where(from_above, fin_in[n, 1, i].astype(jnp.float32), 0.0)
            out[i] = total.astype(jnp.bfloat16)

    keys_all().wait_send()
    for d in range(1, Z):
        for n in range(1, 4):
            z_copy(n, d).wait_send()
    for d in range(1, C):
        for n in range(2):
            s_copy(n, d).wait_send()
            u_copy(n, d).wait_send()
        k_copy(d).wait_send()
        rk_copy(d).wait_send()
        for n in range(SPLITS):
            v_copy(d, n).wait_send()
            rv_copy(d, n).wait_send()
    for n in range(2):
        for s in range(STEPS):
            for way, half in ring_order[: PARTS if s == STEPS - 1 else 2 * PARTS]:
                pl.when(ring_sent(s, way, half))(lambda: ring(n, s, way, half).wait_send())
            for way, half in ring_order[: PARTS if s == 0 else 2 * PARTS]:

                @pl.when(rs_sent(s, way, half))
                def _():
                    if s < STEPS - 1:
                        rs_copy(n, s, way, half).wait_send()
                    else:
                        for m in range(C // PARTS):
                            last_copy(n, way, half, m).wait_send()


def whole(sel, k, v, q, g):
    vmem = pl.BlockSpec(memory_space=pltpu.VMEM)
    bf16 = lambda *shape: pltpu.VMEM(shape, jnp.bfloat16)
    f32 = lambda *shape: pltpu.VMEM(shape, jnp.float32)
    dma = lambda *shape: pltpu.SemaphoreType.DMA(shape)
    units = (C, UNITS, ROWS, HEAD_SIZE)
    table = (BLOCKS, ROWS, HEAD_SIZE)
    heads = (Z, BLOCK_TOKENS, HEAD_SIZE)
    steps = (2, 2, STEPS, PARTS, PIECE, ROWS, HEAD_SIZE)
    return pl.pallas_call(
        whole_kernel,
        out_shape=(
            jax.ShapeDtypeStruct((Z * BLOCK_TOKENS, WIDE), jnp.bfloat16),
            jax.ShapeDtypeStruct(heads, jnp.bfloat16),
            jax.ShapeDtypeStruct(heads, jnp.bfloat16),
        ),
        in_specs=[pl.BlockSpec(memory_space=pltpu.SMEM)] + [vmem] * 3 + [pl.BlockSpec(memory_space=pl.ANY)] * 2,
        out_specs=[vmem] * 3,
        scratch_shapes=[bf16(*heads)] * 2
        + [bf16(Z, BLOCK_TOKENS, WIDE)] * 2
        + [bf16(*table)] * 2
        + [bf16(*units)] * 6
        + [bf16(REQUESTS, ROWS, HEAD_SIZE)] * 2
        + [bf16(Z, KEYS, WIDE), bf16(KEYS, WIDE)]
        + [f32(*heads)] * 2
        + [f32(REQUESTS + 8, ROWS, HEAD_SIZE)]
        + [bf16(*steps)] * 2
        + [bf16(2, SHARE, ROWS, HEAD_SIZE)]
        + [bf16(2, 3, *heads)]
        + [pltpu.VMEM((8, SLOTS), jnp.int32), pltpu.SMEM((8, SLOTS), jnp.int32)]
        + [dma(4, Z)] * 2
        + [dma(2, C)] * 2
        + [dma(2, STEPS, 2, PARTS)] * 2
        + [dma(C)] * 2
        + [dma(C, SPLITS)] * 4
        + [dma(C)] * 2
        + [dma(2, 2, STEPS, PARTS)] * 2
        + [dma(2, C)] * 2
        + [dma(5)]
        + [dma(2)]
        + [dma(2, 2, C)] * 2
        + [pltpu.SemaphoreType.REGULAR((3,))],
        compiler_params=pltpu.CompilerParams(
            vmem_limit_bytes=VMEM, collective_id=0, has_side_effects=True
        ),
        name="whole",
    )(sel, sel, k, v, q, g)


def finish_kernel(dq, dk, dv, dq_out, dk_out, dv_out):
    dq_out[...] = dq[...]
    dk_out[...] = dk[...]
    dv_out[...] = dv[...]


def finish(*arrays):
    vmem = pl.BlockSpec(memory_space=pltpu.VMEM)
    return pl.pallas_call(
        finish_kernel,
        out_shape=tuple(jax.ShapeDtypeStruct(a.shape, a.dtype) for a in arrays),
        in_specs=[vmem] * len(arrays),
        out_specs=[vmem] * len(arrays),
        compiler_params=pltpu.CompilerParams(vmem_limit_bytes=VMEM),
        name="finish",
    )(*arrays)


def body(query, keys, values, output_cotangent, select):
    by_slot = select.reshape(BLOCKS, CHOSEN_BLOCKS).T
    dq, dk, dv = finish(*whole(by_slot, keys, values, query, output_cotangent))
    rows = (Z * BLOCK_TOKENS, HEAD_SIZE)
    return dq, dk.reshape(rows), dv.reshape(rows)


def solution(mesh):
    groups = mesh.shape["grp"]
    grid = jax.sharding.Mesh(
        mesh.devices.reshape(-1, STRIPES, groups), ("y", "xc", "grp")
    )
    rows = ("y", "xc")
    in_specs = (P(rows + ("grp",), None),) * 4 + (P(None, "grp", None),)
    out_specs = (P(rows, "grp"),) * 3
    return jax.shard_map(
        body, mesh=grid, in_specs=in_specs, out_specs=out_specs, check_vma=False
    )
```
